256 devices in a mesh: row: 64 (over x, y, z_lo), col: 4 (over z_hi, core).
Axes of the slice: x: 4, y: 4, z: 8 (z_hi: 2, z_lo: 4; z = z_hi * 4 + z_lo), core: 2. Of those that a mesh axis runs over, the one named last changes fastest.
Arguments:
- pair: bfloat16 [256, 256, 128], P('row', 'col'), may hold values from -6 to 6
- atoms: bfloat16 [8192, 128], P('row'), may hold values from -6 to 6
- atom_token: int32 [8192], P('row'), may hold values from 0 to 255, never falling along the last dimension, each value on 1 to 64 neighbouring positions
- tri_proj: bfloat16 [128, 640], replicated, may hold values from -0.5 to 0.5
- tri_out: bfloat16 [128, 128], replicated, may hold values from -0.5 to 0.5
- w_qkv: bfloat16 [128, 384], replicated, may hold values from -0.5 to 0.5
- w_attn_out: bfloat16 [128, 128], replicated, may hold values from -0.5 to 0.5
- w_token: bfloat16 [128, 384], replicated, may hold values from -0.5 to 0.5
- w_row: bfloat16 [384, 128], replicated, may hold values from -0.3125 to 0.3125
- w_col: bfloat16 [384, 128], replicated, may hold values from -0.3125 to 0.3125
Outputs:
- pair_out: bfloat16 [256, 256, 128], P('row', 'col')
- atom_out: bfloat16 [8192, 128], P('row')
The draws below stay inside these ranges and needn't reach their ends.
Inputs may be any that keep to these rules, and one draw needn't show every extreme that they name: `atom_token`: never falling along atoms; each of the 256 tokens owns 1 to 64 consecutive atoms, one token exactly 64.
All inputs are finite; a program needn't handle non-finite values.
Results may differ from the reference program's by a relative error of at most 0.009.
Values may be sent and summed in bfloat16 or wider, within the bound.
A program may use at most 64 MiB of HBM per device.

```python
import math
import jax
import jax.numpy as jnp
import numpy as np
from jax import lax

C = 128
CA = 128
CS = 384
HEADS = 4
MOST = 64
NT = 256
ATOMS = 8192


def block_levels(rng, shape, shards, least, top_value):
    factor_of = 1.0
    for axis_at, shards_of in shards:
        steps = jax.random.uniform(jax.random.fold_in(jax.random.fold_in(rng, 6), axis_at), (shards_of,), jnp.float32, least / len(shards), top_value / len(shards))
        factor_of = factor_of * jnp.repeat(jnp.exp(steps), shape[axis_at] // shards_of).reshape((-1,) + (1,) * (len(shape) - 1 - axis_at))
    return factor_of


def profile(amount, total, reach, skew):
    weights = [(1 << 20) // math.isqrt(standing ** skew) + 1 for standing in range(2, amount + 1)]
    rest, given = total - reach - (amount - 1), [1] * (amount - 1)
    while rest > 0:
        movable = [i for i in range(amount - 1) if given[i] < reach]
        whole, remaining = sum([weights[i] for i in movable]), rest
        for i in movable:
            more = min(reach - given[i], max(1, remaining * weights[i] // whole), rest)
            given[i] = given[i] + more
            rest = rest - more
    return np.array([reach] + given)


def ragged_sizes(own_key, amount, total, reach, lean):
    if amount == 2:
        one = jax.random.randint(own_key, (), max(1, total - reach), min(reach, total - 1) + 1)
        return jnp.stack([one, total - one])
    sizes = jnp.asarray(profile(amount, total, reach, lean), jnp.int32)
    couples = (amount - 1) // 2
    source_of, taker = sizes[1:1 + 2 * couples:2], sizes[2:2 + 2 * couples:2]
    margin = jnp.minimum(source_of - 1, reach - taker)
    shifted = jax.random.randint(jax.random.fold_in(own_key, 1), (couples,), 0, 1 << 20) % (margin + 1)
    sizes = sizes.at[1:1 + 2 * couples:2].set(source_of - shifted).at[2:2 + 2 * couples:2].set(taker + shifted)
    return sizes[jax.random.permutation(jax.random.fold_in(own_key, 2), amount)]


def bell_draw(own_key, dims, spread, limit, cuts=(), kind=jnp.bfloat16):
    level = block_levels(own_key, dims, cuts, -0.22, 0.18) if cuts else 1.0
    entries = jax.random.normal(own_key, dims, jnp.float32) * spread * level
    return jnp.minimum(jnp.maximum(entries, -limit), limit).astype(kind)


def setup_inputs(seed: int = 0) -> dict:
    splits = jax.random.split(jax.random.key(seed), 11)
    return {
        "pair": bell_draw(splits[0], (NT, NT, C), 1.0, 6.0, ((0, 64), (1, 4))),
        "atoms": bell_draw(splits[1], (ATOMS, CA), 1.0, 6.0, ((0, 64),)),
        "atom_token": jnp.searchsorted(jnp.cumsum(ragged_sizes(splits[2], NT, ATOMS, MOST, 2)), jnp.arange(ATOMS), side="right").astype(jnp.int32),
        "tri_proj": bell_draw(splits[3], (C, 5 * C), C ** -0.5, 0.5),
        "tri_out": bell_draw(splits[4], (C, C), C ** -0.5, 0.5),
        "w_qkv": bell_draw(splits[5], (CA, 3 * CA), CA ** -0.5, 0.5),
        "w_attn_out": bell_draw(splits[6], (CA, CA), CA ** -0.5, 0.5),
        "w_token": bell_draw(splits[7], (CA, CS), CA ** -0.5, 0.5),
        "w_row": bell_draw(splits[8], (CS, C), CS ** -0.5, 0.3125),
        "w_col": bell_draw(splits[9], (CS, C), CS ** -0.5, 0.3125),
    }


def layer_norm(values):
    mean = lax.optimization_barrier(jnp.mean(values, axis=-1, keepdims=True))
    centered = values - mean
    variance = lax.optimization_barrier(jnp.mean(centered * centered, axis=-1, keepdims=True))
    return centered / jnp.sqrt(variance + 1e-05)

def window_attend(queries, keys, values, total):
    count = queries.shape[0] // 32
    width = queries.shape[1]
    query_blocks = queries.astype(jnp.float32).reshape(count, 32, HEADS, width // HEADS)
    key_blocks = keys.astype(jnp.float32).reshape(count + 3, 32, width)
    value_blocks = values.astype(jnp.float32).reshape(count + 3, 32, width)
    key_win = jnp.concatenate([key_blocks[s:s + count] for s in range(4)], axis=1).reshape(count, 128, HEADS, width // HEADS)
    value_win = jnp.concatenate([value_blocks[s:s + count] for s in range(4)], axis=1).reshape(count, 128, HEADS, width // HEADS)
    scores = jnp.einsum('wqhd,wkhd->whqk', query_blocks, key_win) * float(width // HEADS) ** (-0.5)
    position = 32 * jnp.arange(count, dtype=jnp.int32)[:, None] + jnp.arange(128, dtype=jnp.int32)[None, :] - 48
    valid = (position >= 0) & (position < total)
    scores = jnp.where(valid[:, None, None, :], scores, -1e+30)
    probs = jax.nn.softmax(scores, axis=-1).astype(jnp.bfloat16)
    attended = jnp.einsum('whqk,wkhd->wqhd', probs.astype(jnp.float32), value_win)
    return attended.astype(jnp.bfloat16).reshape(count * 32, width)

def reference(pair, atoms, atom_token, tri_proj, tri_out, w_qkv, w_attn_out, w_token, w_row, w_col):
    atom_norm = layer_norm(atoms.astype(jnp.float32)).astype(jnp.bfloat16)
    qkv = jnp.dot(atom_norm, w_qkv, preferred_element_type=jnp.float32).astype(jnp.bfloat16)
    queries = qkv[:, :CA]
    rim = jnp.zeros((48, CA), jnp.bfloat16)
    keys = jnp.concatenate([rim, qkv[:, CA:2 * CA], rim], axis=0)
    values = jnp.concatenate([rim, qkv[:, 2 * CA:], rim], axis=0)
    attended = window_attend(queries, keys, values, ATOMS)
    atom_out = (atoms.astype(jnp.float32) + jnp.dot(attended, w_attn_out, preferred_element_type=jnp.float32)).astype(jnp.bfloat16)
    hidden = jax.nn.relu(jnp.dot(atom_out, w_token, preferred_element_type=jnp.float32))
    token_sum = jax.ops.segment_sum(hidden, atom_token, num_segments=NT)
    token_count = jax.ops.segment_sum(jnp.ones((ATOMS,), jnp.float32), atom_token, num_segments=NT)
    single = (token_sum / token_count[:, None]).astype(jnp.bfloat16)
    pair_norm = layer_norm(pair.astype(jnp.float32)).astype(jnp.bfloat16)
    proj = jnp.dot(pair_norm.reshape(NT * NT, C), tri_proj, preferred_element_type=jnp.float32).reshape(NT, NT, 5 * C)
    left = (jax.nn.sigmoid(proj[..., :C]) * proj[..., C:2 * C]).astype(jnp.bfloat16)
    right = (jax.nn.sigmoid(proj[..., 2 * C:3 * C]) * proj[..., 3 * C:4 * C]).astype(jnp.bfloat16)
    gate = jax.nn.sigmoid(proj[..., 4 * C:])
    tri = jnp.einsum('ikc,jkc->ijc', left.astype(jnp.float32), right.astype(jnp.float32))
    tri_norm = layer_norm(tri).astype(jnp.bfloat16)
    update = gate * jnp.dot(tri_norm.reshape(NT * NT, C), tri_out, preferred_element_type=jnp.float32).reshape(NT, NT, C)
    rows_term = jnp.dot(single, w_row, preferred_element_type=jnp.float32)
    cols_term = jnp.dot(single, w_col, preferred_element_type=jnp.float32)
    pair_out = (pair.astype(jnp.float32) + update + rows_term[:, None, :] + cols_term[None, :, :]).astype(jnp.bfloat16)
    return (pair_out, atom_out)
```

```python
import functools

import jax
import jax.numpy as jnp
from jax import lax
from jax.experimental import pallas as pl
from jax.experimental.pallas import tpu as pltpu
from jax.sharding import PartitionSpec as P

MESH = pl.DeviceIdType.MESH
F32 = jnp.float32
BF16 = jnp.bfloat16
HEADS = 4
C = 128


def normed(values):
    mean = jnp.mean(values, axis=-1, keepdims=True)
    centered = values - mean
    variance = jnp.mean(centered * centered, axis=-1, keepdims=True)
    return centered * lax.rsqrt(variance + 1e-05)


def sigmoid(values):
    return 0.5 * jnp.tanh(0.5 * values) + 0.5


def dot(a, b):
    return jnp.dot(a, b, preferred_element_type=F32)


def dot_nt(a, b):
    return lax.dot_general(a, b, (((1,), (1,)), ((), ())), preferred_element_type=F32)


def halves(low, high):
    lane = lax.broadcasted_iota(jnp.int32, low.shape, 1)
    even = jnp.where(lane < 64, low, pltpu.roll(high, 64, 1))
    odd = jnp.where(lane < 64, pltpu.roll(low, 64, 1), high)
    return even, odd


def kernel(
    pair_ref, atoms_ref, token_ref, tri_proj_ref, tri_out_ref, w_qkv_ref, w_attn_ref, w_token_ref,
    w_row_ref, w_col_ref, pair_out_ref, atom_out_ref,
    wide, send1, recv1, left, right, rights, send3, recv3, gate_ref, upd_ref,
    before, after, tok_send, tok_recv, x_send, x_recv, tot_ref, k_send, k_recv, r_send, r_recv,
    s_halo, r_halo, s_1, r_1, s_2, r_2, s_l, r_l, s_3, r_3, s_t, r_t, s_x, r_x, s_k, r_k, s_r, r_r,
):
    row, col = lax.axis_index("row"), lax.axis_index("col")
    x, p = row // 16, row % 16
    y, z_lo = p // 4, p % 4
    z_hi, core = col // 2, col % 2
    z = z_hi * 4 + z_lo
    group = z_hi * 16 + p
    parity = x % 2

    def plane(g):
        return (x * 16 + g % 16, 2 * (g // 16) + core)

    def next_row():
        carry_y = (z_lo + 1) // 4
        carry_x = (y + carry_y) // 4
        z_to = (z + 1) % 8
        row_to = ((x + carry_x) % 4) * 16 + ((y + carry_y) % 4) * 4 + z_to % 4
        return (row_to, 2 * (z_to // 4) + core)

    def prev_row():
        carry_y = (4 - z_lo) // 4
        carry_x = (3 - y + carry_y) // 4
        z_to = (z + 7) % 8
        row_to = ((x + 4 - carry_x) % 4) * 16 + ((y + 4 - carry_y) % 4) * 4 + z_to % 4
        return (row_to, 2 * (z_to // 4) + core)

    def along_x(step, core_to):
        return (((x + step) % 4) * 16 + p, 2 * z_hi + core_to)

    def token_peer(t):
        z_to = (z + 7 + (t % 4 + 9 - z) % 4) % 8
        return (x * 16 + (t // 4) * 4 + z_to % 4, 2 * (z_to // 4) + core)

    mate = (row, 2 * z_hi + 1 - core)
    flipped = (col * 16 + p, x)
    diagonal = x == col
    own_right = parity == core

    def remote(src, dst, send_sem, recv_sem, to):
        return pltpu.make_async_remote_copy(
            src_ref=src, dst_ref=dst, send_sem=send_sem, recv_sem=recv_sem, device_id=to, device_id_type=MESH
        )

    barrier = pltpu.get_barrier_semaphore()

    def hello(to):
        pl.semaphore_signal(barrier, inc=1, device_id=to, device_id_type=MESH)

    hello(next_row())
    hello(prev_row())

    @pl.loop(1, 32)
    def _(step):
        hello(plane((group + step) % 32))

    @pl.loop(1, 4)
    def _(step):
        hello(along_x(step, 0))
        hello(along_x(step, 1))

    hello(mate)

    @pl.when(jnp.logical_not(diagonal))
    def _():
        hello(flipped)

    pair_norm = normed(pair_ref[...].reshape(256, C).astype(F32)).astype(BF16)
    for side in range(2):
        at = 2 * side * C
        gated = sigmoid(dot(pair_norm, tri_proj_ref[:, at : at + C])) * dot(
            pair_norm, tri_proj_ref[:, at + C : at + 2 * C]
        )
        for half in range(2):
            flat = gated[half * 128 : half * 128 + 128].T
            for slot in range(4):
                wide[pl.ds(side * 8 + slot * 2 + half, 32, stride=16), :] = flat[slot * 32 : slot * 32 + 32]
    send1[...] = wide[...].reshape(32, 16, C).astype(BF16)
    recv1[pl.ds(group, 1)] = send1[pl.ds(group, 1)]
    tot_ref[...] = jnp.ones_like(tot_ref)

    pl.semaphore_wait(barrier, 2 + 31 + 6 + 1 + jnp.where(diagonal, 0, 1))

    to_next = remote(atoms_ref.at[pl.ds(80, 48)], before, s_halo.at[0], r_halo.at[0], next_row())
    to_prev = remote(atoms_ref.at[pl.ds(0, 48)], after, s_halo.at[1], r_halo.at[1], prev_row())
    to_next.start()
    to_prev.start()

    @pl.loop(1, 32)
    def _(step):
        to = (group + step) % 32
        remote(send1.at[to], recv1.at[group], s_1, r_1, plane(to)).start()

    gate_ref[...] = sigmoid(dot(pair_norm, tri_proj_ref[:, 4 * C :]))

    to_next.wait_recv()
    to_prev.wait_recv()
    atoms = atoms_ref[...].astype(F32)
    padded = jnp.concatenate([before[...].astype(F32), atoms, after[...].astype(F32)], axis=0)
    atom_norm = normed(padded).astype(BF16)
    qkv = dot(atom_norm, w_qkv_ref[...]).astype(BF16)
    head_of = lax.broadcasted_iota(jnp.int32, (32, C), 1) // 32
    attended = []
    for window in range(4):
        at = 32 * window
        query = qkv[48 + at : 80 + at, :C]
        query = jnp.concatenate(
            [jnp.where(head_of == h, query, jnp.zeros_like(query)) for h in range(HEADS)], axis=0
        )
        scores = dot_nt(query, qkv[at : at + 128, C : 2 * C]) * (32.0**-0.5)
        position = row * 128 + at - 48 + lax.broadcasted_iota(jnp.int32, (128, 128), 1)
        scores = jnp.where((position >= 0) & (position < 8192), scores, -1e30)
        probs = jnp.exp(scores - jnp.max(scores, axis=-1, keepdims=True))
        probs = (probs / jnp.sum(probs, axis=-1, keepdims=True)).astype(BF16)
        mixed = dot(probs, qkv[at : at + 128, 2 * C :])
        result = mixed[0:32]
        for h in range(1, HEADS):
            result = jnp.where(head_of == h, mixed[32 * h : 32 * h + 32], result)
        attended.append(result)
    attended = jnp.concatenate(attended, axis=0).astype(BF16)
    atom_out = (atoms + dot(attended, w_attn_ref[...])).astype(BF16)
    atom_out_ref[...] = atom_out
    hidden = jnp.maximum(dot(atom_out, w_token_ref[...]), 0.0).astype(BF16)
    summed = jnp.concatenate(
        [hidden[:, :C], hidden[:, C : 2 * C], hidden[:, 2 * C :], jnp.ones((128, C), BF16)], axis=0
    )
    line = lax.broadcasted_iota(jnp.int32, (256, 128), 0)
    to = line // 16
    z_to = (z + 7 + (to % 4 + 9 - z) % 4) % 8
    token_id = 64 * (2 * (z_to // 4) + core) + 4 * to + line % 4
    mine = token_id == token_ref[...]
    part = (line // 4) % 4
    picked = jnp.concatenate(
        [jnp.where(mine & (part == k), 1.0, 0.0).astype(BF16) for k in range(4)], axis=1
    )
    tok_send[...] = dot(picked, summed).reshape(16, 16, C)
    tok_recv[pl.ds(p, 1)] = tok_send[pl.ds(p, 1)]

    @pl.loop(1, 16)
    def _(step):
        t = (p + step) % 16
        remote(tok_send.at[t], tok_recv.at[p], s_t, r_t, token_peer(t)).start()

    remote(send1.at[pl.ds(0, 31)], recv1.at[pl.ds(0, 31)], s_1, r_1, mate).wait_recv()
    wide[...] = recv1[...].reshape(512, C).astype(F32)
    for side in (1, 0):
        for slot in range(4):
            for half in range(2):
                at = side * 8 + slot * 2 + half
                even, odd = halves(
                    wide[pl.ds(at, 16, stride=16), :], wide[pl.ds(256 + at, 16, stride=16), :]
                )
                both = jnp.concatenate([even, odd], axis=0).astype(BF16)
                if side:
                    right[slot, half * 32 : half * 32 + 32, :] = both
                else:
                    left[core, slot, half * 32 : half * 32 + 32, :] = both
        if side:
            place = (x // 2) * 2 + core

            @pl.when(own_right)
            def _():
                rights[pl.ds(place, 1)] = right[...][None]

            @pl.when(jnp.logical_not(own_right))
            def _():
                remote(right, rights.at[place], s_2.at[0], r_2.at[place], along_x(0, parity)).start()

            for step in range(1, 4):
                remote(right, rights.at[place], s_2.at[step], r_2.at[place], along_x(step, parity)).start()
    to_mate = remote(left.at[core], left.at[core], s_l, r_l, mate)
    to_mate.start()

    remote(tok_send.at[pl.ds(0, 15)], tok_recv.at[pl.ds(0, 15)], s_t, r_t, mate).wait_recv()
    x_send[...] = jnp.sum(tok_recv[...], axis=0)
    x_recv[pl.ds(x, 1)] = x_send[...][None]
    for step in range(1, 4):
        remote(x_send, x_recv.at[x], s_x, r_x, along_x(step, core)).start()

    remote(left.at[1 - core], left.at[1 - core], s_l, r_l, mate).wait_recv()
    for place in range(4):

        @pl.when(jnp.logical_not(own_right & ((x // 2) * 2 + core == place)))
        def _():
            remote(right, rights.at[place], s_2.at[0], r_2.at[place], mate).wait_recv()

    for slot in range(4):
        tri = None
        for k in range(2):
            other = jnp.concatenate([rights[k, slot], rights[2 + k, slot]], axis=0)
            term = dot_nt(left[k, slot], other)
            tri = term if tri is None else tri + term
        for half in range(2):
            first, second = halves(tri[half * 32 : half * 32 + 16], tri[half * 32 + 16 : half * 32 + 32])
            at = slot * 2 + half
            wide[pl.ds(at, 16, stride=8), :] = first
            wide[pl.ds(128 + at, 16, stride=8), :] = second
    send3[...] = wide[0:256, :].reshape(32, 8, C).astype(BF16)
    recv3[pl.ds(group, 1)] = send3[pl.ds(group, 1)]

    @pl.loop(1, 32)
    def _(step):
        to = (group + step) % 32
        remote(send3.at[to], recv3.at[group], s_3, r_3, plane(to)).start()

    remote(tok_recv.at[pl.ds(0, 3)], x_recv.at[pl.ds(0, 3)], s_x, r_x, mate).wait_recv()
    tot_ref[0:16, :] = jnp.sum(x_recv[...], axis=0)
    count = tot_ref[12:20, :]
    single = jnp.concatenate([tot_ref[4 * k : 4 * k + 8, :] / count for k in range(3)], axis=1).astype(BF16)
    k_send[...] = dot(single, w_col_ref[...])
    r_send[...] = dot(single, w_row_ref[...])
    k_recv[pl.ds(p, 1)] = k_send[...][None]

    @pl.when(diagonal)
    def _():
        r_recv[...] = r_send[...]

    @pl.when(jnp.logical_not(diagonal))
    def _():
        remote(r_send, r_recv, s_r, r_r, flipped).start()

    @pl.loop(1, 16)
    def _(step):
        to = z_hi * 16 + (p + step) % 16
        remote(k_send, k_recv.at[p], s_k, r_k, plane(to)).start()

    remote(send3.at[pl.ds(0, 31)], recv3.at[pl.ds(0, 31)], s_3, r_3, mate).wait_recv()
    wide[0:256, :] = recv3[...].reshape(256, C).astype(F32)
    for half in range(2):
        tri = jnp.concatenate(
            [wide[pl.ds(slot * 2 + half, 32, stride=8), :] for slot in range(4)], axis=0
        )
        centered = tri - jnp.mean(tri, axis=0, keepdims=True)
        variance = jnp.mean(centered * centered, axis=0, keepdims=True)
        tri_norm = (centered * lax.rsqrt(variance + 1e-05)).T.astype(BF16)
        update = dot(tri_norm, tri_out_ref[...])
        for odd in range(2):
            for i in range(4):
                upd_ref[pl.ds((half * 2 + odd) * 64 + i, 16, stride=4), :] = update[
                    odd * 64 + i * 16 : odd * 64 + i * 16 + 16
                ]
    update = pair_ref[...].reshape(256, C).astype(F32) + upd_ref[...] * gate_ref[...]

    remote(tok_recv.at[pl.ds(0, 15), pl.ds(0, 8)], k_recv.at[pl.ds(0, 15)], s_k, r_k, mate).wait_recv()

    @pl.when(jnp.logical_not(diagonal))
    def _():
        remote(r_send, r_recv, s_r, r_r, flipped).wait_recv()

    k_term = k_recv[...][:, 0:4, :].reshape(64, C)
    for i in range(4):
        pair_out_ref[i] = (update[i * 64 : i * 64 + 64] + k_term + r_recv[i : i + 1, :]).astype(BF16)

    to_next.wait_send()
    to_prev.wait_send()
    to_mate.wait_send()
    remote(send1.at[pl.ds(0, 31)], recv1.at[pl.ds(0, 31)], s_1, r_1, mate).wait_send()
    remote(tok_send.at[pl.ds(0, 15)], tok_recv.at[pl.ds(0, 15)], s_t, r_t, mate).wait_send()
    remote(send3.at[pl.ds(0, 31)], recv3.at[pl.ds(0, 31)], s_3, r_3, mate).wait_send()
    remote(x_recv.at[pl.ds(0, 3)], x_recv.at[pl.ds(0, 3)], s_x, r_x, mate).wait_send()
    remote(k_recv.at[pl.ds(0, 15)], k_recv.at[pl.ds(0, 15)], s_k, r_k, mate).wait_send()
    for step in range(1, 4):
        remote(right, rights.at[0], s_2.at[step], r_2.at[0], mate).wait_send()

    @pl.when(jnp.logical_not(own_right))
    def _():
        remote(right, rights.at[0], s_2.at[0], r_2.at[0], mate).wait_send()

    @pl.when(jnp.logical_not(diagonal))
    def _():
        remote(r_send, r_recv, s_r, r_r, flipped).wait_send()


def per_device(
    pair, atoms, atom_token, tri_proj, tri_out, w_qkv, w_attn_out, w_token, w_row, w_col
):
    vmem = pl.BlockSpec(memory_space=pltpu.VMEM)
    sem = pltpu.SemaphoreType.DMA
    return pl.pallas_call(
        kernel,
        out_shape=(
            jax.ShapeDtypeStruct(pair.shape, BF16),
            jax.ShapeDtypeStruct(atoms.shape, BF16),
        ),
        in_specs=[vmem] * 10,
        out_specs=(vmem, vmem),
        scratch_shapes=[
            pltpu.VMEM((512, C), F32),
            pltpu.VMEM((32, 16, C), BF16),
            pltpu.VMEM((32, 16, C), BF16),
            pltpu.VMEM((2, 4, 64, C), BF16),
            pltpu.VMEM((4, 64, C), BF16),
            pltpu.VMEM((4, 4, 64, C), BF16),
            pltpu.VMEM((32, 8, C), BF16),
            pltpu.VMEM((32, 8, C), BF16),
            pltpu.VMEM((256, C), F32),
            pltpu.VMEM((256, C), F32),
            pltpu.VMEM((48, C), BF16),
            pltpu.VMEM((48, C), BF16),
            pltpu.VMEM((16, 16, C), F32),
            pltpu.VMEM((16, 16, C), F32),
            pltpu.VMEM((16, C), F32),
            pltpu.VMEM((4, 16, C), F32),
            pltpu.VMEM((24, C), F32),
            pltpu.VMEM((8, C), F32),
            pltpu.VMEM((16, 8, C), F32),
            pltpu.VMEM((8, C), F32),
            pltpu.VMEM((8, C), F32),
            sem((2,)), sem((2,)),
            sem, sem,
            sem((4,)), sem((4,)),
            sem, sem,
            sem, sem,
            sem, sem,
            sem, sem,
            sem, sem,
            sem, sem,
        ],
        compiler_params=pltpu.CompilerParams(
            collective_id=0, has_side_effects=True, vmem_limit_bytes=32 << 20
        ),
    )(
        pair, atoms, atom_token.reshape(1, 128), tri_proj, tri_out, w_qkv, w_attn_out, w_token,
        w_row, w_col,
    )


def solution(mesh):
    return jax.shard_map(
        per_device,
        mesh=mesh,
        in_specs=(
            P("row", "col", None),
            P("row", None),
            P("row"),
            P(),
            P(),
            P(),
            P(),
            P(),
            P(),
            P(),
        ),
        out_specs=(P("row", "col", None), P("row", None)),
        check_vma=False,
    )
```

```python
import functools

import jax
import jax.numpy as jnp
from jax import lax
from jax.experimental import pallas as pl
from jax.experimental.pallas import tpu as pltpu
from jax.sharding import PartitionSpec as P

MESH = pl.DeviceIdType.MESH
F32 = jnp.float32
BF16 = jnp.bfloat16
HEADS = 4
C = 128


def normed(values):
    mean = jnp.mean(values, axis=-1, keepdims=True)
    centered = values - mean
    variance = jnp.mean(centered * centered, axis=-1, keepdims=True)
    return centered * lax.rsqrt(variance + 1e-05)


def sigmoid(values):
    return 0.5 * jnp.tanh(0.5 * values) + 0.5


def dot(a, b):
    return jnp.dot(a, b, preferred_element_type=F32)


def dot_nt(a, b):
    return lax.dot_general(a, b, (((1,), (1,)), ((), ())), preferred_element_type=F32)


def halves(low, high):
    lane = lax.broadcasted_iota(jnp.int32, low.shape, 1)
    even = jnp.where(lane < 64, low, pltpu.roll(high, 64, 1))
    odd = jnp.where(lane < 64, pltpu.roll(low, 64, 1), high)
    return even, odd


def kernel(
    pair_in, atoms_in, token_in, tri_proj_in, tri_out_in, w_qkv_in, w_attn_in, w_token_in, w_row_in,
    w_col_in, pair_out_ref, atom_out_ref,
    pair_ref, atoms_ref, token_ref, tri_proj_ref, tri_out_ref, w_qkv_ref, w_attn_ref, w_token_ref,
    w_row_ref, w_col_ref,
    wide, send1, recv1, left, right, rights, send3, recv3, gate_ref, upd_ref,
    before, after, tok_send, tok_recv, x_send, x_recv, tot_ref, k_send, k_recv, r_send, r_recv,
    s_halo, r_halo, s_1, r_1, s_2, r_2, s_l, r_l, s_3, r_3, s_t, r_t, s_x, r_x, s_k, r_k, s_r, r_r,
    s_in,
):
    row, col = lax.axis_index("row"), lax.axis_index("col")
    x, p = row // 16, row % 16
    y, z_lo = p // 4, p % 4
    z_hi, core = col // 2, col % 2
    z = z_hi * 4 + z_lo
    group = z_hi * 16 + p
    parity = x % 2

    def plane(g):
        return (x * 16 + g % 16, 2 * (g // 16) + core)

    def next_row():
        carry_y = (z_lo + 1) // 4
        carry_x = (y + carry_y) // 4
        z_to = (z + 1) % 8
        row_to = ((x + carry_x) % 4) * 16 + ((y + carry_y) % 4) * 4 + z_to % 4
        return (row_to, 2 * (z_to // 4) + core)

    def prev_row():
        carry_y = (4 - z_lo) // 4
        carry_x = (3 - y + carry_y) // 4
        z_to = (z + 7) % 8
        row_to = ((x + 4 - carry_x) % 4) * 16 + ((y + 4 - carry_y) % 4) * 4 + z_to % 4
        return (row_to, 2 * (z_to // 4) + core)

    def along_x(step, core_to):
        return (((x + step) % 4) * 16 + p, 2 * z_hi + core_to)

    def token_peer(t):
        z_to = (z + 7 + (t % 4 + 9 - z) % 4) % 8
        return (x * 16 + (t // 4) * 4 + z_to % 4, 2 * (z_to // 4) + core)

    mate = (row, 2 * z_hi + 1 - core)
    flipped = (col * 16 + p, x)
    diagonal = x == col
    own_right = parity == core

    def remote(src, dst, send_sem, recv_sem, to):
        return pltpu.make_async_remote_copy(
            src_ref=src, dst_ref=dst, send_sem=send_sem, recv_sem=recv_sem, device_id=to, device_id_type=MESH
        )

    arguments = [
        pltpu.make_async_copy(source, target, s_in.at[k])
        for k, (source, target) in enumerate(
            (
                (pair_in, pair_ref),
                (tri_proj_in, tri_proj_ref),
                (atoms_in, atoms_ref),
                (w_qkv_in, w_qkv_ref),
                (w_attn_in, w_attn_ref),
                (w_token_in, w_token_ref),
                (token_in, token_ref),
                (tri_out_in, tri_out_ref),
                (w_row_in, w_row_ref),
                (w_col_in, w_col_ref),
            )
        )
    ]
    for k in range(3):
        arguments[k].start()

    barrier = pltpu.get_barrier_semaphore()

    def hello(to):
        pl.semaphore_signal(barrier, inc=1, device_id=to, device_id_type=MESH)

    hello(next_row())
    hello(prev_row())

    @pl.loop(1, 32)
    def _(step):
        hello(plane((group + step) % 32))

    @pl.loop(1, 4)
    def _(step):
        hello(along_x(step, 0))
        hello(along_x(step, 1))

    hello(mate)

    @pl.when(jnp.logical_not(diagonal))
    def _():
        hello(flipped)

    for k in range(3, 10):
        arguments[k].start()

    arguments[0].wait()
    arguments[1].wait()
    pair_norm = normed(pair_ref[...].reshape(256, C).astype(F32)).astype(BF16)
    for side in range(2):
        at = 2 * side * C
        gated = sigmoid(dot(pair_norm, tri_proj_ref[:, at : at + C])) * dot(
            pair_norm, tri_proj_ref[:, at + C : at + 2 * C]
        )
        for half in range(2):
            flat = gated[half * 128 : half * 128 + 128].T
            for slot in range(4):
                wide[pl.ds(side * 8 + slot * 2 + half, 32, stride=16), :] = flat[slot * 32 : slot * 32 + 32]
    send1[...] = wide[...].reshape(32, 16, C).astype(BF16)
    recv1[pl.ds(group, 1)] = send1[pl.ds(group, 1)]
    tot_ref[...] = jnp.ones_like(tot_ref)

    pl.semaphore_wait(barrier, 2 + 31 + 6 + 1 + jnp.where(diagonal, 0, 1))

    arguments[2].wait()
    to_next = remote(atoms_ref.at[pl.ds(80, 48)], before, s_halo.at[0], r_halo.at[0], next_row())
    to_prev = remote(atoms_ref.at[pl.ds(0, 48)], after, s_halo.at[1], r_halo.at[1], prev_row())
    to_next.start()
    to_prev.start()

    @pl.loop(1, 32)
    def _(step):
        to = (group + step) % 32
        remote(send1.at[to], recv1.at[group], s_1, r_1, plane(to)).start()

    gate_ref[...] = sigmoid(dot(pair_norm, tri_proj_ref[:, 4 * C :]))

    for k in range(3, 7):
        arguments[k].wait()
    to_next.wait_recv()
    to_prev.wait_recv()
    atoms = atoms_ref[...].astype(F32)
    padded = jnp.concatenate([before[...].astype(F32), atoms, after[...].astype(F32)], axis=0)
    atom_norm = normed(padded).astype(BF16)
    qkv = dot(atom_norm, w_qkv_ref[...]).astype(BF16)
    head_of = lax.broadcasted_iota(jnp.int32, (32, C), 1) // 32
    attended = []
    for window in range(4):
        at = 32 * window
        query = qkv[48 + at : 80 + at, :C]
        query = jnp.concatenate(
            [jnp.where(head_of == h, query, jnp.zeros_like(query)) for h in range(HEADS)], axis=0
        )
        scores = dot_nt(query, qkv[at : at + 128, C : 2 * C]) * (32.0**-0.5)
        position = row * 128 + at - 48 + lax.broadcasted_iota(jnp.int32, (128, 128), 1)
        scores = jnp.where((position >= 0) & (position < 8192), scores, -1e30)
        probs = jnp.exp(scores - jnp.max(scores, axis=-1, keepdims=True))
        probs = (probs / jnp.sum(probs, axis=-1, keepdims=True)).astype(BF16)
        mixed = dot(probs, qkv[at : at + 128, 2 * C :])
        result = mixed[0:32]
        for h in range(1, HEADS):
            result = jnp.where(head_of == h, mixed[32 * h : 32 * h + 32], result)
        attended.append(result)
    attended = jnp.concatenate(attended, axis=0).astype(BF16)
    atom_out = (atoms + dot(attended, w_attn_ref[...])).astype(BF16)
    atom_out_ref[...] = atom_out
    hidden = jnp.maximum(dot(atom_out, w_token_ref[...]), 0.0).astype(BF16)
    summed = jnp.concatenate(
        [hidden[:, :C], hidden[:, C : 2 * C], hidden[:, 2 * C :], jnp.ones((128, C), BF16)], axis=0
    )
    line = lax.broadcasted_iota(jnp.int32, (256, 128), 0)
    to = line // 16
    z_to = (z + 7 + (to % 4 + 9 - z) % 4) % 8
    token_id = 64 * (2 * (z_to // 4) + core) + 4 * to + line % 4
    mine = token_id == token_ref[...]
    part = (line // 4) % 4
    picked = jnp.concatenate(
        [jnp.where(mine & (part == k), 1.0, 0.0).astype(BF16) for k in range(4)], axis=1
    )
    tok_send[...] = dot(picked, summed).reshape(16, 16, C)
    tok_recv[pl.ds(p, 1)] = tok_send[pl.ds(p, 1)]

    @pl.loop(1, 16)
    def _(step):
        t = (p + step) % 16
        remote(tok_send.at[t], tok_recv.at[p], s_t, r_t, token_peer(t)).start()

    remote(send1.at[pl.ds(0, 31)], recv1.at[pl.ds(0, 31)], s_1, r_1, mate).wait_recv()
    wide[...] = recv1[...].reshape(512, C).astype(F32)
    for side in (1, 0):
        for slot in range(4):
            for half in range(2):
                at = side * 8 + slot * 2 + half
                even, odd = halves(
                    wide[pl.ds(at, 16, stride=16), :], wide[pl.ds(256 + at, 16, stride=16), :]
                )
                both = jnp.concatenate([even, odd], axis=0).astype(BF16)
                if side:
                    right[slot, half * 32 : half * 32 + 32, :] = both
                else:
                    left[core, slot, half * 32 : half * 32 + 32, :] = both
        if side:
            place = (x // 2) * 2 + core

            @pl.when(own_right)
            def _():
                rights[pl.ds(place, 1)] = right[...][None]

            @pl.when(jnp.logical_not(own_right))
            def _():
                remote(right, rights.at[place], s_2.at[0], r_2.at[place], along_x(0, parity)).start()

            for step in range(1, 4):
                remote(right, rights.at[place], s_2.at[step], r_2.at[place], along_x(step, parity)).start()
    to_mate = remote(left.at[core], left.at[core], s_l, r_l, mate)
    to_mate.start()

    remote(tok_send.at[pl.ds(0, 15)], tok_recv.at[pl.ds(0, 15)], s_t, r_t, mate).wait_recv()
    x_send[...] = jnp.sum(tok_recv[...], axis=0)
    x_recv[pl.ds(x, 1)] = x_send[...][None]
    for step in range(1, 4):
        remote(x_send, x_recv.at[x], s_x, r_x, along_x(step, core)).start()

    remote(left.at[1 - core], left.at[1 - core], s_l, r_l, mate).wait_recv()
    for place in range(4):

        @pl.when(jnp.logical_not(own_right & ((x // 2) * 2 + core == place)))
        def _():
            remote(right, rights.at[place], s_2.at[0], r_2.at[place], mate).wait_recv()

    for slot in range(4):
        tri = None
        for k in range(2):
            other = jnp.concatenate([rights[k, slot], rights[2 + k, slot]], axis=0)
            term = dot_nt(left[k, slot], other)
            tri = term if tri is None else tri + term
        for half in range(2):
            first, second = halves(tri[half * 32 : half * 32 + 16], tri[half * 32 + 16 : half * 32 + 32])
            at = slot * 2 + half
            wide[pl.ds(at, 16, stride=8), :] = first
            wide[pl.ds(128 + at, 16, stride=8), :] = second
    send3[...] = wide[0:256, :].reshape(32, 8, C).astype(BF16)
    recv3[pl.ds(group, 1)] = send3[pl.ds(group, 1)]

    @pl.loop(1, 32)
    def _(step):
        to = (group + step) % 32
        remote(send3.at[to], recv3.at[group], s_3, r_3, plane(to)).start()

    for k in range(7, 10):
        arguments[k].wait()

    remote(tok_recv.at[pl.ds(0, 3)], x_recv.at[pl.ds(0, 3)], s_x, r_x, mate).wait_recv()
    tot_ref[0:16, :] = jnp.sum(x_recv[...], axis=0)
    count = tot_ref[12:20, :]
    single = jnp.concatenate([tot_ref[4 * k : 4 * k + 8, :] / count for k in range(3)], axis=1).astype(BF16)
    k_send[...] = dot(single, w_col_ref[...])
    r_send[...] = dot(single, w_row_ref[...])
    k_recv[pl.ds(p, 1)] = k_send[...][None]

    @pl.when(diagonal)
    def _():
        r_recv[...] = r_send[...]

    @pl.when(jnp.logical_not(diagonal))
    def _():
        remote(r_send, r_recv, s_r, r_r, flipped).start()

    @pl.loop(1, 16)
    def _(step):
        to = z_hi * 16 + (p + step) % 16
        remote(k_send, k_recv.at[p], s_k, r_k, plane(to)).start()

    remote(send3.at[pl.ds(0, 31)], recv3.at[pl.ds(0, 31)], s_3, r_3, mate).wait_recv()
    wide[0:256, :] = recv3[...].reshape(256, C).astype(F32)
    for half in range(2):
        tri = jnp.concatenate(
            [wide[pl.ds(slot * 2 + half, 32, stride=8), :] for slot in range(4)], axis=0
        )
        centered = tri - jnp.mean(tri, axis=0, keepdims=True)
        variance = jnp.mean(centered * centered, axis=0, keepdims=True)
        tri_norm = (centered * lax.rsqrt(variance + 1e-05)).T.astype(BF16)
        update = dot(tri_norm, tri_out_ref[...])
        for odd in range(2):
            for i in range(4):
                upd_ref[pl.ds((half * 2 + odd) * 64 + i, 16, stride=4), :] = update[
                    odd * 64 + i * 16 : odd * 64 + i * 16 + 16
                ]
    update = pair_ref[...].reshape(256, C).astype(F32) + upd_ref[...] * gate_ref[...]

    remote(tok_recv.at[pl.ds(0, 15), pl.ds(0, 8)], k_recv.at[pl.ds(0, 15)], s_k, r_k, mate).wait_recv()

    @pl.when(jnp.logical_not(diagonal))
    def _():
        remote(r_send, r_recv, s_r, r_r, flipped).wait_recv()

    k_term = k_recv[...][:, 0:4, :].reshape(64, C)
    for i in range(4):
        pair_out_ref[i] = (update[i * 64 : i * 64 + 64] + k_term + r_recv[i : i + 1, :]).astype(BF16)

    to_next.wait_send()
    to_prev.wait_send()
    to_mate.wait_send()
    remote(send1.at[pl.ds(0, 31)], recv1.at[pl.ds(0, 31)], s_1, r_1, mate).wait_send()
    remote(tok_send.at[pl.ds(0, 15)], tok_recv.at[pl.ds(0, 15)], s_t, r_t, mate).wait_send()
    remote(send3.at[pl.ds(0, 31)], recv3.at[pl.ds(0, 31)], s_3, r_3, mate).wait_send()
    remote(x_recv.at[pl.ds(0, 3)], x_recv.at[pl.ds(0, 3)], s_x, r_x, mate).wait_send()
    remote(k_recv.at[pl.ds(0, 15)], k_recv.at[pl.ds(0, 15)], s_k, r_k, mate).wait_send()
    for step in range(1, 4):
        remote(right, rights.at[0], s_2.at[step], r_2.at[0], mate).wait_send()

    @pl.when(jnp.logical_not(own_right))
    def _():
        remote(right, rights.at[0], s_2.at[0], r_2.at[0], mate).wait_send()

    @pl.when(jnp.logical_not(diagonal))
    def _():
        remote(r_send, r_recv, s_r, r_r, flipped).wait_send()


def per_device(
    pair, atoms, atom_token, tri_proj, tri_out, w_qkv, w_attn_out, w_token, w_row, w_col
):
    vmem = pl.BlockSpec(memory_space=pltpu.VMEM)
    sem = pltpu.SemaphoreType.DMA
    return pl.pallas_call(
        kernel,
        out_shape=(
            jax.ShapeDtypeStruct(pair.shape, BF16),
            jax.ShapeDtypeStruct(atoms.shape, BF16),
        ),
        in_specs=[pl.BlockSpec(memory_space=pltpu.HBM)] * 10,
        out_specs=(vmem, vmem),
        scratch_shapes=[
            pltpu.VMEM(pair.shape, BF16),
            pltpu.VMEM(atoms.shape, BF16),
            pltpu.VMEM((1, 128), jnp.int32),
            pltpu.VMEM(tri_proj.shape, BF16),
            pltpu.VMEM(tri_out.shape, BF16),
            pltpu.VMEM(w_qkv.shape, BF16),
            pltpu.VMEM(w_attn_out.shape, BF16),
            pltpu.VMEM(w_token.shape, BF16),
            pltpu.VMEM(w_row.shape, BF16),
            pltpu.VMEM(w_col.shape, BF16),
            pltpu.VMEM((512, C), F32),
            pltpu.VMEM((32, 16, C), BF16),
            pltpu.VMEM((32, 16, C), BF16),
            pltpu.VMEM((2, 4, 64, C), BF16),
            pltpu.VMEM((4, 64, C), BF16),
            pltpu.VMEM((4, 4, 64, C), BF16),
            pltpu.VMEM((32, 8, C), BF16),
            pltpu.VMEM((32, 8, C), BF16),
            pltpu.VMEM((256, C), F32),
            pltpu.VMEM((256, C), F32),
            pltpu.VMEM((48, C), BF16),
            pltpu.VMEM((48, C), BF16),
            pltpu.VMEM((16, 16, C), F32),
            pltpu.VMEM((16, 16, C), F32),
            pltpu.VMEM((16, C), F32),
            pltpu.VMEM((4, 16, C), F32),
            pltpu.VMEM((24, C), F32),
            pltpu.VMEM((8, C), F32),
            pltpu.VMEM((16, 8, C), F32),
            pltpu.VMEM((8, C), F32),
            pltpu.VMEM((8, C), F32),
            sem((2,)), sem((2,)),
            sem, sem,
            sem((4,)), sem((4,)),
            sem, sem,
            sem, sem,
            sem, sem,
            sem, sem,
            sem, sem,
            sem, sem,
            sem((10,)),
        ],
        compiler_params=pltpu.CompilerParams(
            collective_id=0, has_side_effects=True, vmem_limit_bytes=60 << 20
        ),
    )(
        pair, atoms, atom_token.reshape(1, 128), tri_proj, tri_out, w_qkv, w_attn_out, w_token,
        w_row, w_col,
    )


def solution(mesh):
    return jax.shard_map(
        per_device,
        mesh=mesh,
        in_specs=(
            P("row", "col", None),
            P("row", None),
            P("row"),
            P(),
            P(),
            P(),
            P(),
            P(),
            P(),
            P(),
        ),
        out_specs=(P("row", "col", None), P("row", None)),
        check_vma=False,
    )
```

```python
import functools

import jax
import jax.numpy as jnp
from jax import lax
from jax.experimental import pallas as pl
from jax.experimental.pallas import tpu as pltpu
from jax.sharding import PartitionSpec as P

MESH = pl.DeviceIdType.MESH
F32 = jnp.float32
BF16 = jnp.bfloat16
HEADS = 4
C = 128


def normed(values):
    mean = jnp.mean(values, axis=-1, keepdims=True)
    centered = values - mean
    variance = jnp.mean(centered * centered, axis=-1, keepdims=True)
    return centered * lax.rsqrt(variance + 1e-05)


def sigmoid(values):
    return 0.5 * jnp.tanh(0.5 * values) + 0.5


def dot(a, b):
    return jnp.dot(a, b, preferred_element_type=F32)


def dot_nt(a, b):
    return lax.dot_general(a, b, (((1,), (1,)), ((), ())), preferred_element_type=F32)


def halves(low, high):
    lane = lax.broadcasted_iota(jnp.int32, low.shape, 1)
    even = jnp.where(lane < 64, low, pltpu.roll(high, 64, 1))
    odd = jnp.where(lane < 64, pltpu.roll(low, 64, 1), high)
    return even, odd


def kernel(
    pair_in, atoms_in, token_in, tri_proj_in, tri_out_in, w_qkv_in, w_attn_in, w_token_in, w_row_in,
    w_col_in, pair_out_ref, atom_out_ref,
    pair_ref, atoms_ref, token_ref, tri_proj_ref, tri_out_ref, w_qkv_ref, w_attn_ref, w_token_ref,
    w_row_ref, w_col_ref,
    wide, send1, recv1, left, right, rights, send3, recv3, gate_ref, upd_ref,
    before, after, tok_send, tok_recv, x_send, x_recv, tot_ref, k_send, k_recv, r_send, r_recv,
    s_halo, r_halo, s_1, r_1, s_2, r_2, s_l, r_l, s_3, r_3, s_t, r_t, s_x, r_x, s_k, r_k, s_r, r_r,
    s_in,
):
    row, col = lax.axis_index("row"), lax.axis_index("col")
    x, p = row // 16, row % 16
    y, z_lo = p // 4, p % 4
    z_hi, core = col // 2, col % 2
    z = z_hi * 4 + z_lo
    group = z_hi * 16 + p
    parity = x % 2

    def plane(g):
        return (x * 16 + g % 16, 2 * (g // 16) + core)

    def next_row():
        carry_y = (z_lo + 1) // 4
        carry_x = (y + carry_y) // 4
        z_to = (z + 1) % 8
        row_to = ((x + carry_x) % 4) * 16 + ((y + carry_y) % 4) * 4 + z_to % 4
        return (row_to, 2 * (z_to // 4) + core)

    def prev_row():
        carry_y = (4 - z_lo) // 4
        carry_x = (3 - y + carry_y) // 4
        z_to = (z + 7) % 8
        row_to = ((x + 4 - carry_x) % 4) * 16 + ((y + 4 - carry_y) % 4) * 4 + z_to % 4
        return (row_to, 2 * (z_to // 4) + core)

    def along_x(step, core_to):
        return (((x + step) % 4) * 16 + p, 2 * z_hi + core_to)

    def token_peer(t):
        z_to = (z + 7 + (t % 4 + 9 - z) % 4) % 8
        return (x * 16 + (t // 4) * 4 + z_to % 4, 2 * (z_to // 4) + core)

    mate = (row, 2 * z_hi + 1 - core)
    flipped = (col * 16 + p, x)
    diagonal = x == col
    own_right = parity == core

    def remote(src, dst, send_sem, recv_sem, to):
        return pltpu.make_async_remote_copy(
            src_ref=src, dst_ref=dst, send_sem=send_sem, recv_sem=recv_sem, device_id=to, device_id_type=MESH
        )

    arguments = [
        pltpu.make_async_copy(source, target, s_in.at[k])
        for k, (source, target) in enumerate(
            (
                (pair_in, pair_ref),
                (tri_proj_in, tri_proj_ref),
                (atoms_in, atoms_ref),
                (w_qkv_in, w_qkv_ref),
                (w_attn_in, w_attn_ref),
                (w_token_in, w_token_ref),
                (token_in, token_ref),
                (tri_out_in, tri_out_ref),
                (w_row_in, w_row_ref),
                (w_col_in, w_col_ref),
            )
        )
    ]
    for k in range(3):
        arguments[k].start()

    barrier = pltpu.get_barrier_semaphore()

    def hello(to):
        pl.semaphore_signal(barrier, inc=1, device_id=to, device_id_type=MESH)

    hello(next_row())
    hello(prev_row())

    @pl.loop(1, 32)
    def _(step):
        hello(plane((group + step) % 32))

    @pl.loop(1, 4)
    def _(step):
        hello(along_x(step, 0))
        hello(along_x(step, 1))

    hello(mate)

    @pl.when(jnp.logical_not(diagonal))
    def _():
        hello(flipped)

    for k in range(3, 10):
        arguments[k].start()

    arguments[0].wait()
    arguments[1].wait()
    pair_norm = normed(pair_ref[...].reshape(256, C).astype(F32)).astype(BF16)
    for side in range(2):
        at = 2 * side * C
        gated = sigmoid(dot(pair_norm, tri_proj_ref[:, at : at + C])) * dot(
            pair_norm, tri_proj_ref[:, at + C : at + 2 * C]
        )
        for half in range(2):
            flat = gated[half * 128 : half * 128 + 128].T
            for slot in range(4):
                wide[pl.ds(side * 8 + slot * 2 + half, 32, stride=16), :] = flat[slot * 32 : slot * 32 + 32]
    send1[...] = wide[...].reshape(32, 16, C).astype(BF16)
    recv1[pl.ds(group, 1)] = send1[pl.ds(group, 1)]
    tot_ref[...] = jnp.ones_like(tot_ref)

    pl.semaphore_wait(barrier, 2 + 31 + 6 + 1 + jnp.where(diagonal, 0, 1))

    arguments[2].wait()
    to_next = remote(atoms_ref.at[pl.ds(80, 48)], before, s_halo.at[0], r_halo.at[0], next_row())
    to_prev = remote(atoms_ref.at[pl.ds(0, 48)], after, s_halo.at[1], r_halo.at[1], prev_row())
    to_next.start()
    to_prev.start()

    @pl.loop(1, 32)
    def _(step):
        to = (group + step) % 32
        remote(send1.at[to], recv1.at[group], s_1, r_1, plane(to)).start()

    gate_ref[...] = sigmoid(dot(pair_norm, tri_proj_ref[:, 4 * C :]))

    for k in range(3, 7):
        arguments[k].wait()
    to_next.wait_recv()
    to_prev.wait_recv()
    atoms = atoms_ref[...].astype(F32)
    padded = jnp.concatenate([before[...].astype(F32), atoms, after[...].astype(F32)], axis=0)
    atom_norm = normed(padded).astype(BF16)
    qkv = dot(atom_norm, w_qkv_ref[...]).astype(BF16)
    head_of = lax.broadcasted_iota(jnp.int32, (32, C), 1) // 32
    attended = []
    for window in range(4):
        at = 32 * window
        query = qkv[48 + at : 80 + at, :C]
        query = jnp.concatenate(
            [jnp.where(head_of == h, query, jnp.zeros_like(query)) for h in range(HEADS)], axis=0
        )
        scores = dot_nt(query, qkv[at : at + 128, C : 2 * C]) * (32.0**-0.5)
        position = row * 128 + at - 48 + lax.broadcasted_iota(jnp.int32, (128, 128), 1)
        scores = jnp.where((position >= 0) & (position < 8192), scores, -1e30)
        probs = jnp.exp(scores - jnp.max(scores, axis=-1, keepdims=True))
        probs = (probs / jnp.sum(probs, axis=-1, keepdims=True)).astype(BF16)
        mixed = dot(probs, qkv[at : at + 128, 2 * C :])
        result = mixed[0:32]
        for h in range(1, HEADS):
            result = jnp.where(head_of == h, mixed[32 * h : 32 * h + 32], result)
        attended.append(result)
    attended = jnp.concatenate(attended, axis=0).astype(BF16)
    atom_out = (atoms + dot(attended, w_attn_ref[...])).astype(BF16)
    atom_out_ref[...] = atom_out
    hidden = jnp.maximum(dot(atom_out, w_token_ref[...]), 0.0).astype(BF16)
    summed = jnp.concatenate(
        [hidden[:, :C], hidden[:, C : 2 * C], hidden[:, 2 * C :], jnp.ones((128, C), BF16)], axis=0
    )
    line = lax.broadcasted_iota(jnp.int32, (256, 128), 0)
    to = line // 16
    z_to = (z + 7 + (to % 4 + 9 - z) % 4) % 8
    token_id = 64 * (2 * (z_to // 4) + core) + 4 * to + line % 4
    mine = token_id == token_ref[...]
    part = (line // 4) % 4
    picked = jnp.concatenate(
        [jnp.where(mine & (part == k), 1.0, 0.0).astype(BF16) for k in range(4)], axis=1
    )
    tok_send[...] = dot(picked, summed).reshape(16, 16, C)
    tok_recv[pl.ds(p, 1)] = tok_send[pl.ds(p, 1)]

    @pl.loop(1, 16)
    def _(step):
        t = (p + step) % 16
        remote(tok_send.at[t], tok_recv.at[p], s_t, r_t, token_peer(t)).start()

    remote(send1.at[pl.ds(0, 31)], recv1.at[pl.ds(0, 31)], s_1, r_1, mate).wait_recv()
    wide[...] = recv1[...].reshape(512, C).astype(F32)
    for side in (1, 0):
        for slot in range(4):
            for half in range(2):
                at = side * 8 + slot * 2 + half
                even, odd = halves(
                    wide[pl.ds(at, 16, stride=16), :], wide[pl.ds(256 + at, 16, stride=16), :]
                )
                both = jnp.concatenate([even, odd], axis=0).astype(BF16)
                if side:
                    right[slot, half * 32 : half * 32 + 32, :] = both
                else:
                    left[core, slot, half * 32 : half * 32 + 32, :] = both
        if side:
            place = (x // 2) * 2 + core

            @pl.when(own_right)
            def _():
                rights[pl.ds(place, 1)] = right[...][None]

            @pl.when(jnp.logical_not(own_right))
            def _():
                remote(right, rights.at[place], s_2.at[0], r_2.at[place], along_x(0, parity)).start()

            for step in range(1, 4):
                remote(right, rights.at[place], s_2.at[step], r_2.at[place], along_x(step, parity)).start()
    to_mate = remote(left.at[core], left.at[core], s_l, r_l, mate)
    to_mate.start()

    remote(tok_send.at[pl.ds(0, 15)], tok_recv.at[pl.ds(0, 15)], s_t, r_t, mate).wait_recv()
    x_send[...] = jnp.sum(tok_recv[...], axis=0)
    x_recv[pl.ds(x, 1)] = x_send[...][None]
    for step in range(1, 4):
        remote(x_send, x_recv.at[x], s_x, r_x, along_x(step, core)).start()

    remote(left.at[1 - core], left.at[1 - core], s_l, r_l, mate).wait_recv()
    for place in range(4):

        @pl.when(jnp.logical_not(own_right & ((x // 2) * 2 + core == place)))
        def _():
            remote(right, rights.at[place], s_2.at[0], r_2.at[place], mate).wait_recv()

    for slot in range(4):
        tri = None
        for k in range(2):
            other = jnp.concatenate([rights[k, slot], rights[2 + k, slot]], axis=0)
            term = dot_nt(left[k, slot], other)
            tri = term if tri is None else tri + term
        for half in range(2):
            first, second = halves(tri[half * 32 : half * 32 + 16], tri[half * 32 + 16 : half * 32 + 32])
            at = slot * 2 + half
            wide[pl.ds(at, 16, stride=8), :] = first
            wide[pl.ds(128 + at, 16, stride=8), :] = second
    send3[...] = wide[0:256, :].reshape(32, 8, C).astype(BF16)
    recv3[pl.ds(group, 1)] = send3[pl.ds(group, 1)]

    @pl.loop(1, 32)
    def _(step):
        to = (group + step) % 32
        remote(send3.at[to], recv3.at[group], s_3, r_3, plane(to)).start()

    for k in range(7, 10):
        arguments[k].wait()

    remote(tok_recv.at[pl.ds(0, 3)], x_recv.at[pl.ds(0, 3)], s_x, r_x, mate).wait_recv()
    tot_ref[0:16, :] = jnp.sum(x_recv[...], axis=0)
    count = tot_ref[12:20, :]
    single = jnp.concatenate([tot_ref[4 * k : 4 * k + 8, :] / count for k in range(3)], axis=1).astype(BF16)
    k_send[...] = dot(single, w_col_ref[...])
    r_send[...] = dot(single, w_row_ref[...])
    k_recv[pl.ds(p, 1)] = k_send[...][None]

    @pl.when(diagonal)
    def _():
        r_recv[...] = r_send[...]

    @pl.when(jnp.logical_not(diagonal))
    def _():
        remote(r_send, r_recv, s_r, r_r, flipped).start()

    @pl.loop(1, 16)
    def _(step):
        to = z_hi * 16 + (p + step) % 16
        remote(k_send, k_recv.at[p], s_k, r_k, plane(to)).start()

    remote(send3.at[pl.ds(0, 31)], recv3.at[pl.ds(0, 31)], s_3, r_3, mate).wait_recv()
    wide[0:256, :] = recv3[...].reshape(256, C).astype(F32)
    for half in range(2):
        tri = jnp.concatenate(
            [wide[pl.ds(slot * 2 + half, 32, stride=8), :] for slot in range(4)], axis=0
        )
        centered = tri - jnp.mean(tri, axis=0, keepdims=True)
        variance = jnp.mean(centered * centered, axis=0, keepdims=True)
        tri_norm = (centered * lax.rsqrt(variance + 1e-05)).T.astype(BF16)
        update = dot(tri_norm, tri_out_ref[...])
        for odd in range(2):
            for i in range(4):
                upd_ref[pl.ds((half * 2 + odd) * 64 + i, 16, stride=4), :] = update[
                    odd * 64 + i * 16 : odd * 64 + i * 16 + 16
                ]
    update = pair_ref[...].reshape(256, C).astype(F32) + upd_ref[...] * gate_ref[...]

    remote(tok_recv.at[pl.ds(0, 15), pl.ds(0, 8)], k_recv.at[pl.ds(0, 15)], s_k, r_k, mate).wait_recv()

    @pl.when(jnp.logical_not(diagonal))
    def _():
        remote(r_send, r_recv, s_r, r_r, flipped).wait_recv()

    k_term = k_recv[...][:, 0:4, :].reshape(64, C)
    for i in range(4):
        pair_out_ref[i] = (update[i * 64 : i * 64 + 64] + k_term + r_recv[i : i + 1, :]).astype(BF16)

    to_next.wait_send()
    to_prev.wait_send()
    to_mate.wait_send()
    remote(send1.at[pl.ds(0, 31)], recv1.at[pl.ds(0, 31)], s_1, r_1, mate).wait_send()
    remote(tok_send.at[pl.ds(0, 15)], tok_recv.at[pl.ds(0, 15)], s_t, r_t, mate).wait_send()
    remote(send3.at[pl.ds(0, 31)], recv3.at[pl.ds(0, 31)], s_3, r_3, mate).wait_send()
    remote(x_recv.at[pl.ds(0, 3)], x_recv.at[pl.ds(0, 3)], s_x, r_x, mate).wait_send()
    remote(k_recv.at[pl.ds(0, 15)], k_recv.at[pl.ds(0, 15)], s_k, r_k, mate).wait_send()
    for step in range(1, 4):
        remote(right, rights.at[0], s_2.at[step], r_2.at[0], mate).wait_send()

    @pl.when(jnp.logical_not(own_right))
    def _():
        remote(right, rights.at[0], s_2.at[0], r_2.at[0], mate).wait_send()

    @pl.when(jnp.logical_not(diagonal))
    def _():
        remote(r_send, r_recv, s_r, r_r, flipped).wait_send()


def store(pair_in, atoms_in, pair_to, atoms_to, done):
    first = pltpu.make_async_copy(pair_in, pair_to, done.at[0])
    second = pltpu.make_async_copy(atoms_in, atoms_to, done.at[1])
    first.start()
    second.start()
    first.wait()
    second.wait()


def per_device(
    pair, atoms, atom_token, tri_proj, tri_out, w_qkv, w_attn_out, w_token, w_row, w_col
):
    vmem = pl.BlockSpec(memory_space=pltpu.VMEM)
    sem = pltpu.SemaphoreType.DMA
    arguments = (
        pair, atoms, atom_token.reshape(1, 128), tri_proj, tri_out, w_qkv, w_attn_out, w_token,
        w_row, w_col,
    )
    results = pl.pallas_call(
        kernel,
        out_shape=(pltpu.VMEM(pair.shape, BF16), pltpu.VMEM(atoms.shape, BF16)),
        in_specs=[pl.BlockSpec(memory_space=pltpu.HBM)] * 10,
        out_specs=(vmem, vmem),
        scratch_shapes=[
            pltpu.VMEM(pair.shape, BF16),
            pltpu.VMEM(atoms.shape, BF16),
            pltpu.VMEM((1, 128), jnp.int32),
            pltpu.VMEM(tri_proj.shape, BF16),
            pltpu.VMEM(tri_out.shape, BF16),
            pltpu.VMEM(w_qkv.shape, BF16),
            pltpu.VMEM(w_attn_out.shape, BF16),
            pltpu.VMEM(w_token.shape, BF16),
            pltpu.VMEM(w_row.shape, BF16),
            pltpu.VMEM(w_col.shape, BF16),
            pltpu.VMEM((512, C), F32),
            pltpu.VMEM((32, 16, C), BF16),
            pltpu.VMEM((32, 16, C), BF16),
            pltpu.VMEM((2, 4, 64, C), BF16),
            pltpu.VMEM((4, 64, C), BF16),
            pltpu.VMEM((4, 4, 64, C), BF16),
            pltpu.VMEM((32, 8, C), BF16),
            pltpu.VMEM((32, 8, C), BF16),
            pltpu.VMEM((256, C), F32),
            pltpu.VMEM((256, C), F32),
            pltpu.VMEM((48, C), BF16),
            pltpu.VMEM((48, C), BF16),
            pltpu.VMEM((16, 16, C), F32),
            pltpu.VMEM((16, 16, C), F32),
            pltpu.VMEM((16, C), F32),
            pltpu.VMEM((4, 16, C), F32),
            pltpu.VMEM((24, C), F32),
            pltpu.VMEM((8, C), F32),
            pltpu.VMEM((16, 8, C), F32),
            pltpu.VMEM((8, C), F32),
            pltpu.VMEM((8, C), F32),
            sem((2,)), sem((2,)),
            sem, sem,
            sem((4,)), sem((4,)),
            sem, sem,
            sem, sem,
            sem, sem,
            sem, sem,
            sem, sem,
            sem, sem,
            sem((10,)),
        ],
        compiler_params=pltpu.CompilerParams(
            collective_id=0, has_side_effects=True, vmem_limit_bytes=32 << 20
        ),
    )(*(pltpu.with_memory_space_constraint(value, pltpu.HBM) for value in arguments))
    hbm = pl.BlockSpec(memory_space=pltpu.HBM)
    return pl.pallas_call(
        store,
        out_shape=(
            jax.ShapeDtypeStruct(pair.shape, BF16),
            jax.ShapeDtypeStruct(atoms.shape, BF16),
        ),
        in_specs=[vmem, vmem],
        out_specs=(hbm, hbm),
        scratch_shapes=[sem((2,))],
    )(*(pltpu.with_memory_space_constraint(value, pltpu.VMEM) for value in results))


def solution(mesh):
    return jax.shard_map(
        per_device,
        mesh=mesh,
        in_specs=(
            P("row", "col", None),
            P("row", None),
            P("row"),
            P(),
            P(),
            P(),
            P(),
            P(),
            P(),
            P(),
        ),
        out_specs=(P("row", "col", None), P("row", None)),
        check_vma=False,
    )
```

```python
import functools

import jax
import jax.numpy as jnp
from jax import lax
from jax.experimental import pallas as pl
from jax.experimental.pallas import tpu as pltpu
from jax.sharding import PartitionSpec as P

MESH = pl.DeviceIdType.MESH
F32 = jnp.float32
BF16 = jnp.bfloat16
HEADS = 4
C = 128


def normed(values):
    mean = jnp.mean(values, axis=-1, keepdims=True)
    centered = values - mean
    variance = jnp.mean(centered * centered, axis=-1, keepdims=True)
    return centered * lax.rsqrt(variance + 1e-05)


def sigmoid(values):
    return 0.5 * jnp.tanh(0.5 * values) + 0.5


def dot(a, b):
    return jnp.dot(a, b, preferred_element_type=F32)


def dot_nt(a, b):
    return lax.dot_general(a, b, (((1,), (1,)), ((), ())), preferred_element_type=F32)


def halves(low, high):
    lane = lax.broadcasted_iota(jnp.int32, low.shape, 1)
    even = jnp.where(lane < 64, low, pltpu.roll(high, 64, 1))
    odd = jnp.where(lane < 64, pltpu.roll(low, 64, 1), high)
    return even, odd


def kernel(
    pair_in, atoms_in, token_in, tri_proj_in, tri_out_in, w_qkv_in, w_attn_in, w_token_in, w_row_in,
    w_col_in, pair_out_ref, atom_out_ref,
    pair_ref, atoms_ref, token_ref, tri_proj_ref, tri_out_ref, w_qkv_ref, w_attn_ref, w_token_ref,
    w_row_ref, w_col_ref,
    wide, send1, recv1, left, right, rights, send3, recv3, gate_ref, upd_ref,
    before, after, tok_send, tok_recv, k_send, k_recv, r_send, r_recv,
    s_halo, r_halo, s_1, r_1, s_2, r_2, s_l, r_l, s_3, r_3, s_t, r_t, s_k, r_k, s_r, r_r,
    s_in, plane_in,
):
    row, col = lax.axis_index("row"), lax.axis_index("col")
    x, p = row // 16, row % 16
    y, z_lo = p // 4, p % 4
    z_hi, core = col // 2, col % 2
    z = z_hi * 4 + z_lo
    group = z_hi * 16 + p
    parity = x % 2

    ys = [(y + step) % 4 for step in range(4)]

    def place_of(x_to, y_to, z_to):
        return (x_to * 16 + y_to * 4 + z_to % 4, 2 * (z_to // 4) + core)

    def plane(act):
        @pl.loop(0, 7)
        def _(k):
            z_to = (z + 4 + ((k + 1) // 2) * (1 - 2 * (k % 2))) % 8
            for step in (2, 1, 3, 0):
                act((z_to // 4) * 16 + ys[step] * 4 + z_to % 4, place_of(x, ys[step], z_to))

        for step in (2, 1, 3):
            act(z_hi * 16 + ys[step] * 4 + z_lo, place_of(x, ys[step], z))

    def other_x(act, z_steps):
        @pl.loop(0, 3)
        def _(k):
            x_to = (x + 2 + ((k + 1) // 2) * (1 - 2 * (k % 2))) % 4
            for z_step in z_steps:
                z_to = (z + z_step) % 8
                for step in (2, 1, 3, 0):
                    act(x_to, ys[step] * 4 + z_to % 4, place_of(x_to, ys[step], z_to))

    def same_x(act, z_steps):
        for z_step in z_steps:
            z_to = (z + z_step) % 8
            for step in (2, 1, 3, 0):
                if step or z_step:
                    act(x, ys[step] * 4 + z_to % 4, place_of(x, ys[step], z_to))

    def next_row():
        carry_y = (z_lo + 1) // 4
        carry_x = (y + carry_y) // 4
        z_to = (z + 1) % 8
        row_to = ((x + carry_x) % 4) * 16 + ((y + carry_y) % 4) * 4 + z_to % 4
        return (row_to, 2 * (z_to // 4) + core)

    def prev_row():
        carry_y = (4 - z_lo) // 4
        carry_x = (3 - y + carry_y) // 4
        z_to = (z + 7) % 8
        row_to = ((x + 4 - carry_x) % 4) * 16 + ((y + 4 - carry_y) % 4) * 4 + z_to % 4
        return (row_to, 2 * (z_to // 4) + core)

    def along_x(step, core_to):
        return (((x + step) % 4) * 16 + p, 2 * z_hi + core_to)

    mate = (row, 2 * z_hi + 1 - core)
    own_right = parity == core

    def remote(src, dst, send_sem, recv_sem, to):
        return pltpu.make_async_remote_copy(
            src_ref=src, dst_ref=dst, send_sem=send_sem, recv_sem=recv_sem, device_id=to, device_id_type=MESH
        )

    arguments = [
        pltpu.make_async_copy(source, target, s_in.at[k])
        for k, (source, target) in enumerate(
            (
                (pair_in, pair_ref),
                (tri_proj_in, tri_proj_ref),
                (atoms_in, atoms_ref),
                (w_qkv_in, w_qkv_ref),
                (w_attn_in, w_attn_ref),
                (w_token_in, w_token_ref),
                (token_in, token_ref),
                (tri_out_in, tri_out_ref),
                (w_row_in, w_row_ref),
                (w_col_in, w_col_ref),
            )
        )
    ]
    for k in range(3):
        arguments[k].start()

    barrier = pltpu.get_barrier_semaphore()

    def hello(to):
        pl.semaphore_signal(barrier, inc=1, device_id=to, device_id_type=MESH)

    plane(lambda group_to, to: hello(to))
    for step in (2, 1, 3):
        hello(along_x(step, core))
        hello(along_x(step, 1 - core))
    hello(next_row())
    hello(prev_row())
    hello(mate)

    for k in range(3, 10):
        arguments[k].start()

    arguments[0].wait()
    arguments[1].wait()
    pair_norm = normed(pair_ref[...].reshape(256, C).astype(F32)).astype(BF16)
    for side in range(2):
        at = 2 * side * C
        gated = sigmoid(dot(pair_norm, tri_proj_ref[:, at : at + C])) * dot(
            pair_norm, tri_proj_ref[:, at + C : at + 2 * C]
        )
        for half in range(2):
            flat = gated[half * 128 : half * 128 + 128].T
            for slot in range(4):
                wide[pl.ds(side * 8 + slot * 2 + half, 32, stride=16), :] = flat[slot * 32 : slot * 32 + 32]
    send1[...] = wide[...].reshape(32, 16, C).astype(BF16)
    recv1[pl.ds(group, 1)] = send1[pl.ds(group, 1)]
    gate_ref[...] = sigmoid(dot(pair_norm, tri_proj_ref[:, 4 * C :]))

    pl.semaphore_wait(barrier, 31 + 6 + 2 + 1)
    for step in (2, 1, 3):
        pl.semaphore_signal(plane_in, inc=1, device_id=along_x(step, core), device_id_type=MESH)

    arguments[2].wait()
    to_next = remote(atoms_ref.at[pl.ds(80, 48)], before, s_halo.at[0], r_halo.at[0], next_row())
    to_prev = remote(atoms_ref.at[pl.ds(0, 48)], after, s_halo.at[1], r_halo.at[1], prev_row())
    to_next.start()
    to_prev.start()

    plane(lambda group_to, to: remote(send1.at[group_to], recv1.at[group], s_1, r_1, to).start())

    for k in range(3, 10):
        arguments[k].wait()
    atoms = atoms_ref[...].astype(F32)
    own = dot(normed(atoms).astype(BF16), w_qkv_ref[...]).astype(BF16)
    line = lax.broadcasted_iota(jnp.int32, (128, 128), 0)
    lane = lax.broadcasted_iota(jnp.int32, (128, 128), 1)
    token_id = 64 * (2 * ((line // 4) % 2) + core) + 4 * (line // 8) + line % 4
    picked = jnp.where(token_id == token_ref[...], 1.0, 0.0).astype(BF16)
    to_next.wait_recv()
    to_prev.wait_recv()
    edge = jnp.concatenate([before[...], after[...]], axis=0).astype(F32)
    edge = dot(normed(edge).astype(BF16), w_qkv_ref[:, C:]).astype(BF16)
    keys = jnp.concatenate([edge[0:48, :C], own[:, C : 2 * C], edge[48:96, :C]], axis=0)
    values = jnp.concatenate([edge[0:48, C:], own[:, 2 * C :], edge[48:96, C:]], axis=0)
    head_of = lax.broadcasted_iota(jnp.int32, (32, C), 1) // 32
    attended = []
    for window in range(4):
        at = 32 * window
        query = own[at : at + 32, :C]
        query = jnp.concatenate(
            [jnp.where(head_of == h, query, jnp.zeros_like(query)) for h in range(HEADS)], axis=0
        )
        scores = dot_nt(query, keys[at : at + 128]) * (32.0**-0.5)
        position = row * 128 + at - 48 + lax.broadcasted_iota(jnp.int32, (128, 128), 1)
        scores = jnp.where((position >= 0) & (position < 8192), scores, -1e30)
        probs = jnp.exp(scores - jnp.max(scores, axis=-1, keepdims=True))
        probs = (probs / jnp.sum(probs, axis=-1, keepdims=True)).astype(BF16)
        mixed = dot(probs, values[at : at + 128])
        result = mixed[0:32]
        for h in range(1, HEADS):
            result = jnp.where(head_of == h, mixed[32 * h : 32 * h + 32], result)
        attended.append(result)
    attended = jnp.concatenate(attended, axis=0).astype(BF16)
    remote(send1.at[pl.ds(0, 31)], recv1.at[pl.ds(0, 31)], s_1, r_1, mate).wait_recv()
    wide[...] = recv1[...].reshape(512, C).astype(F32)
    place = (x // 2) * 2 + core

    def assemble(side, slot):
        for half in range(2):
            at = side * 8 + slot * 2 + half
            even, odd = halves(
                wide[pl.ds(at, 16, stride=16), :], wide[pl.ds(256 + at, 16, stride=16), :]
            )
            both = jnp.concatenate([even, odd], axis=0).astype(BF16)
            if side:
                right[slot, half * 32 : half * 32 + 32, :] = both
            else:
                left[core, slot, half * 32 : half * 32 + 32, :] = both

    def pass_right(part, step):
        return remote(
            right.at[pl.ds(2 * part, 2)], rights.at[place, pl.ds(2 * part, 2)],
            s_2.at[2 * step + part], r_2.at[2 * place + part], along_x(step, parity),
        )

    for part in range(2):
        assemble(1, 2 * part)
        assemble(1, 2 * part + 1)
        for step in (2, 1, 3):
            pass_right(part, step).start()

        @pl.when(jnp.logical_not(own_right))
        def _():
            pass_right(part, 0).start()

    atom_out = (atoms + dot(attended, w_attn_ref[...])).astype(BF16)
    atom_out_ref[...] = atom_out
    hidden = jnp.maximum(dot(atom_out, w_token_ref[...]), 0.0).astype(BF16)
    summed = dot(picked, hidden).astype(BF16)
    count = jnp.broadcast_to(jnp.sum(picked.astype(F32), axis=1, keepdims=True), (128, C))
    count = jnp.where(lane < 64, pltpu.roll(count.reshape(16, 8, C), 4, 1).reshape(128, C), count)
    k_part = dot(summed, w_col_ref[...])
    r_part = dot(summed, w_row_ref[...])
    r_swap = pltpu.roll(r_part.reshape(16, 8, C), 4, 1).reshape(128, C)
    for high, part in ((0, r_part), (1, r_swap)):
        part = jnp.where(line % 8 < 4, part, count)
        tok_send[high] = jnp.concatenate(
            [k_part.reshape(16, 8, C), part.reshape(16, 8, C)], axis=1
        ).astype(BF16)
    tok_recv[pl.ds(row, 1)] = tok_send[pl.ds(x // 2, 1), pl.ds(p, 1)].reshape(1, 16, C)

    pl.semaphore_wait(plane_in, 3)

    def give(x_to, piece, to):
        remote(tok_send.at[x_to // 2, piece], tok_recv.at[row], s_t, r_t, to).start()

    other_x(give, (2, 7, 1, 0))
    same_x(give, (2, 7, 1, 0))

    @pl.when(own_right)
    def _():
        rights[pl.ds(place, 1)] = right[...][None]

    for slot in range(4):
        assemble(0, slot)
    to_mate = remote(left.at[core], left.at[core], s_l, r_l, mate)
    to_mate.start()

    remote(left.at[1 - core], left.at[1 - core], s_l, r_l, mate).wait_recv()
    for slot in range(4):
        if slot % 2 == 0:
            for source in range(4):

                @pl.when(jnp.logical_not(own_right & (place == source)))
                def _():
                    remote(
                        right.at[pl.ds(slot, 2)], rights.at[source, pl.ds(slot, 2)],
                        s_2.at[0], r_2.at[2 * source + slot // 2], mate,
                    ).wait_recv()

        tri = None
        for k in range(2):
            other = jnp.concatenate([rights[k, slot], rights[2 + k, slot]], axis=0)
            term = dot_nt(left[k, slot], other)
            tri = term if tri is None else tri + term
        for half in range(2):
            first, second = halves(tri[half * 32 : half * 32 + 16], tri[half * 32 + 16 : half * 32 + 32])
            at = slot * 2 + half
            wide[pl.ds(at, 16, stride=8), :] = first
            wide[pl.ds(128 + at, 16, stride=8), :] = second
    send3[...] = wide[0:256, :].reshape(32, 8, C).astype(BF16)
    recv3[pl.ds(group, 1)] = send3[pl.ds(group, 1)]

    plane(lambda group_to, to: remote(send3.at[group_to], recv3.at[group], s_3, r_3, to).start())

    remote(tok_recv.at[pl.ds(0, 63)], tok_recv.at[pl.ds(0, 63)], s_t, r_t, mate).wait_recv()
    total = jnp.sum(tok_recv[...].astype(F32), axis=0)
    count = total[8:16]
    swap = pltpu.roll(count, 64, 1)
    lane, line = lane[0:8], line[0:8]
    low = pltpu.roll(jnp.where(lane < 64, count, swap), 4, 0)
    high = jnp.where(lane < 64, swap, count)
    k_send[...] = total[0:8] / jnp.where(line < 4, low, high)
    k_recv[pl.ds(p, 1)] = k_send[...][None]
    same_x(lambda x_to, piece, to: remote(k_send, k_recv.at[p], s_k, r_k, to).start(), (2, 7, 1, 0))
    count = jnp.where(x // 2 == 0, low, pltpu.roll(high, 4, 0))
    r_send[...] = total[8:16] / jnp.where(line < 4, count, 1.0)

    @pl.when(own_right)
    def _():
        r_recv[...] = r_send[...]
        remote(r_send, r_recv, s_r, r_r, mate).start()

    remote(send3.at[pl.ds(0, 31)], recv3.at[pl.ds(0, 31)], s_3, r_3, mate).wait_recv()
    wide[0:256, :] = recv3[...].reshape(256, C).astype(F32)
    for half in range(2):
        tri = jnp.concatenate(
            [wide[pl.ds(slot * 2 + half, 32, stride=8), :] for slot in range(4)], axis=0
        )
        centered = tri - jnp.mean(tri, axis=0, keepdims=True)
        variance = jnp.mean(centered * centered, axis=0, keepdims=True)
        tri_norm = (centered * lax.rsqrt(variance + 1e-05)).T.astype(BF16)
        update = dot(tri_norm, tri_out_ref[...])
        for odd in range(2):
            for i in range(4):
                upd_ref[pl.ds((half * 2 + odd) * 64 + i, 16, stride=4), :] = update[
                    odd * 64 + i * 16 : odd * 64 + i * 16 + 16
                ]
    update = pair_ref[...].reshape(256, C).astype(F32) + upd_ref[...] * gate_ref[...]

    remote(k_recv.at[pl.ds(0, 15)], k_recv.at[pl.ds(0, 15)], s_k, r_k, mate).wait_recv()

    @pl.when(jnp.logical_not(own_right))
    def _():
        remote(r_send, r_recv, s_r, r_r, mate).wait_recv()

    k_term = k_recv[...]
    k_term = jnp.where(z_hi == 0, k_term[:, 0:4], k_term[:, 4:8]).reshape(64, C)
    r_term = r_recv[...]
    for i in range(4):
        pair_out_ref[i] = (update[i * 64 : i * 64 + 64] + k_term + r_term[i : i + 1]).astype(BF16)

    to_next.wait_send()
    to_prev.wait_send()
    to_mate.wait_send()
    remote(send1.at[pl.ds(0, 31)], recv1.at[pl.ds(0, 31)], s_1, r_1, mate).wait_send()
    remote(tok_recv.at[pl.ds(0, 63)], tok_recv.at[pl.ds(0, 63)], s_t, r_t, mate).wait_send()
    remote(send3.at[pl.ds(0, 31)], recv3.at[pl.ds(0, 31)], s_3, r_3, mate).wait_send()
    remote(k_recv.at[pl.ds(0, 15)], k_recv.at[pl.ds(0, 15)], s_k, r_k, mate).wait_send()
    for part in range(2):
        for step in range(1, 4):
            pass_right(part, step).wait_send()

        @pl.when(jnp.logical_not(own_right))
        def _():
            pass_right(part, 0).wait_send()

    @pl.when(own_right)
    def _():
        remote(r_send, r_recv, s_r, r_r, mate).wait_send()


def store(pair_in, atoms_in, pair_to, atoms_to, done):
    first = pltpu.make_async_copy(pair_in, pair_to, done.at[0])
    second = pltpu.make_async_copy(atoms_in, atoms_to, done.at[1])
    first.start()
    second.start()
    first.wait()
    second.wait()


def per_device(
    pair, atoms, atom_token, tri_proj, tri_out, w_qkv, w_attn_out, w_token, w_row, w_col
):
    vmem = pl.BlockSpec(memory_space=pltpu.VMEM)
    sem = pltpu.SemaphoreType.DMA
    arguments = (
        pair, atoms, atom_token.reshape(1, 128), tri_proj, tri_out, w_qkv, w_attn_out, w_token,
        w_row, w_col,
    )
    results = pl.pallas_call(
        kernel,
        out_shape=(pltpu.VMEM(pair.shape, BF16), pltpu.VMEM(atoms.shape, BF16)),
        in_specs=[pl.BlockSpec(memory_space=pltpu.HBM)] * 10,
        out_specs=(vmem, vmem),
        scratch_shapes=[
            pltpu.VMEM(pair.shape, BF16),
            pltpu.VMEM(atoms.shape, BF16),
            pltpu.VMEM((1, 128), jnp.int32),
            pltpu.VMEM(tri_proj.shape, BF16),
            pltpu.VMEM(tri_out.shape, BF16),
            pltpu.VMEM(w_qkv.shape, BF16),
            pltpu.VMEM(w_attn_out.shape, BF16),
            pltpu.VMEM(w_token.shape, BF16),
            pltpu.VMEM(w_row.shape, BF16),
            pltpu.VMEM(w_col.shape, BF16),
            pltpu.VMEM((512, C), F32),
            pltpu.VMEM((32, 16, C), BF16),
            pltpu.VMEM((32, 16, C), BF16),
            pltpu.VMEM((2, 4, 64, C), BF16),
            pltpu.VMEM((4, 64, C), BF16),
            pltpu.VMEM((4, 4, 64, C), BF16),
            pltpu.VMEM((32, 8, C), BF16),
            pltpu.VMEM((32, 8, C), BF16),
            pltpu.VMEM((256, C), F32),
            pltpu.VMEM((256, C), F32),
            pltpu.VMEM((48, C), BF16),
            pltpu.VMEM((48, C), BF16),
            pltpu.VMEM((2, 16, 16, C), BF16),
            pltpu.VMEM((64, 16, C), BF16),
            pltpu.VMEM((8, C), F32),
            pltpu.VMEM((16, 8, C), F32),
            pltpu.VMEM((8, C), F32),
            pltpu.VMEM((8, C), F32),
            sem((2,)), sem((2,)),
            sem, sem,
            sem((8,)), sem((8,)),
            sem, sem,
            sem, sem,
            sem, sem,
            sem, sem,
            sem, sem,
            sem((10,)),
            pltpu.SemaphoreType.REGULAR,
        ],
        compiler_params=pltpu.CompilerParams(
            collective_id=0, has_side_effects=True, vmem_limit_bytes=32 << 20
        ),
    )(*(pltpu.with_memory_space_constraint(value, pltpu.HBM) for value in arguments))
    hbm = pl.BlockSpec(memory_space=pltpu.HBM)
    return pl.pallas_call(
        store,
        out_shape=(
            jax.ShapeDtypeStruct(pair.shape, BF16),
            jax.ShapeDtypeStruct(atoms.shape, BF16),
        ),
        in_specs=[vmem, vmem],
        out_specs=(hbm, hbm),
        scratch_shapes=[sem((2,))],
    )(*(pltpu.with_memory_space_constraint(value, pltpu.VMEM) for value in results))


def solution(mesh):
    return jax.shard_map(
        per_device,
        mesh=mesh,
        in_specs=(
            P("row", "col", None),
            P("row", None),
            P("row"),
            P(),
            P(),
            P(),
            P(),
            P(),
            P(),
            P(),
        ),
        out_specs=(P("row", "col", None), P("row", None)),
        check_vma=False,
    )
```

```python
import functools

import jax
import jax.numpy as jnp
from jax import lax
from jax.experimental import pallas as pl
from jax.experimental.pallas import tpu as pltpu
from jax.sharding import PartitionSpec as P

MESH = pl.DeviceIdType.MESH
F32 = jnp.float32
BF16 = jnp.bfloat16
HEADS = 4
C = 128


def normed(values):
    mean = jnp.mean(values, axis=-1, keepdims=True)
    centered = values - mean
    variance = jnp.mean(centered * centered, axis=-1, keepdims=True)
    return centered * lax.rsqrt(variance + 1e-05)


def sigmoid(values):
    return 0.5 * jnp.tanh(0.5 * values) + 0.5


def dot(a, b):
    return jnp.dot(a, b, preferred_element_type=F32)


def dot_nt(a, b):
    return lax.dot_general(a, b, (((1,), (1,)), ((), ())), preferred_element_type=F32)


def halves(low, high):
    lane = lax.broadcasted_iota(jnp.int32, low.shape, 1)
    even = jnp.where(lane < 64, low, pltpu.roll(high, 64, 1))
    odd = jnp.where(lane < 64, pltpu.roll(low, 64, 1), high)
    return even, odd


def kernel(
    pair_in, atoms_in, token_in, tri_proj_in, tri_out_in, w_qkv_in, w_attn_in, w_token_in, w_row_in,
    w_col_in, pair_out_ref, atom_out_ref,
    pair_ref, atoms_ref, token_ref, tri_proj_ref, tri_out_ref, w_qkv_ref, w_attn_ref, w_token_ref,
    w_row_ref, w_col_ref,
    wide, send1, recv1, left, right, rights, send3, recv3, gate_ref, upd_ref,
    before, after, token_before, token_after, tok_send, tok_recv, k_send, k_recv, r_recv,
    s_halo, r_halo, s_1, r_1, s_2, r_2, s_l, r_l, s_3, r_3, s_t, r_t, s_k, r_k, s_r, r_r,
    s_in, plane_in,
):
    row, col = lax.axis_index("row"), lax.axis_index("col")
    x, p = row // 16, row % 16
    y, z_lo = p // 4, p % 4
    z_hi, core = col // 2, col % 2
    z = z_hi * 4 + z_lo
    group = z_hi * 16 + p
    parity = x % 2

    ys = [(y + step) % 4 for step in range(4)]

    def place_of(x_to, y_to, z_to):
        return (x_to * 16 + y_to * 4 + z_to % 4, 2 * (z_to // 4) + core)

    def plane(act):
        @pl.loop(0, 7)
        def _(k):
            z_to = (z + 4 + ((k + 1) // 2) * (1 - 2 * (k % 2))) % 8
            for step in (2, 1, 3, 0):
                act((z_to // 4) * 16 + ys[step] * 4 + z_to % 4, place_of(x, ys[step], z_to))

        for step in (2, 1, 3):
            act(z_hi * 16 + ys[step] * 4 + z_lo, place_of(x, ys[step], z))

    def other_x(act, z_steps):
        @pl.loop(0, 3)
        def _(k):
            x_to = (x + 2 + ((k + 1) // 2) * (1 - 2 * (k % 2))) % 4
            for z_step in z_steps:
                z_to = (z + z_step) % 8
                for step in (2, 1, 3, 0):
                    act(x_to, ys[step] * 4 + z_to % 4, place_of(x_to, ys[step], z_to))

    def same_x(act, z_steps):
        for z_step in z_steps:
            z_to = (z + z_step) % 8
            for step in (2, 1, 3, 0):
                if step or z_step:
                    act(x, ys[step] * 4 + z_to % 4, place_of(x, ys[step], z_to))

    def next_row():
        carry_y = (z_lo + 1) // 4
        carry_x = (y + carry_y) // 4
        z_to = (z + 1) % 8
        row_to = ((x + carry_x) % 4) * 16 + ((y + carry_y) % 4) * 4 + z_to % 4
        return (row_to, 2 * (z_to // 4) + core)

    def prev_row():
        carry_y = (4 - z_lo) // 4
        carry_x = (3 - y + carry_y) // 4
        z_to = (z + 7) % 8
        row_to = ((x + 4 - carry_x) % 4) * 16 + ((y + 4 - carry_y) % 4) * 4 + z_to % 4
        return (row_to, 2 * (z_to // 4) + core)

    def along_x(step, core_to):
        return (((x + step) % 4) * 16 + p, 2 * z_hi + core_to)

    mate = (row, 2 * z_hi + 1 - core)
    own_right = parity == core

    def remote(src, dst, send_sem, recv_sem, to):
        return pltpu.make_async_remote_copy(
            src_ref=src, dst_ref=dst, send_sem=send_sem, recv_sem=recv_sem, device_id=to, device_id_type=MESH
        )

    arguments = [
        pltpu.make_async_copy(source, target, s_in.at[k])
        for k, (source, target) in enumerate(
            (
                (pair_in, pair_ref),
                (tri_proj_in, tri_proj_ref),
                (atoms_in, atoms_ref),
                (w_qkv_in, w_qkv_ref),
                (w_attn_in, w_attn_ref),
                (w_token_in, w_token_ref),
                (token_in, token_ref),
                (tri_out_in, tri_out_ref),
                (w_row_in, w_row_ref),
                (w_col_in, w_col_ref),
            )
        )
    ]
    for k in range(3):
        arguments[k].start()

    barrier = pltpu.get_barrier_semaphore()

    def hello(to):
        pl.semaphore_signal(barrier, inc=1, device_id=to, device_id_type=MESH)

    plane(lambda group_to, to: hello(to))
    for step in (2, 1, 3):
        hello(along_x(step, core))
        hello(along_x(step, 1 - core))
    hello(next_row())
    hello(prev_row())
    hello(mate)

    for k in range(3, 10):
        arguments[k].start()

    arguments[0].wait()
    arguments[1].wait()
    pair_norm = normed(pair_ref[...].reshape(256, C).astype(F32)).astype(BF16)
    for side in range(2):
        at = 2 * side * C
        gated = sigmoid(dot(pair_norm, tri_proj_ref[:, at : at + C])) * dot(
            pair_norm, tri_proj_ref[:, at + C : at + 2 * C]
        )
        for half in range(2):
            flat = gated[half * 128 : half * 128 + 128].T
            for slot in range(4):
                wide[pl.ds(side * 8 + slot * 2 + half, 32, stride=16), :] = flat[slot * 32 : slot * 32 + 32]
    send1[...] = wide[...].reshape(32, 16, C).astype(BF16)
    recv1[pl.ds(group, 1)] = send1[pl.ds(group, 1)]
    gate_ref[...] = sigmoid(dot(pair_norm, tri_proj_ref[:, 4 * C :]))

    pl.semaphore_wait(barrier, 31 + 6 + 2 + 1)
    for step in (2, 1, 3):
        pl.semaphore_signal(plane_in, inc=1, device_id=along_x(step, core), device_id_type=MESH)

    arguments[2].wait()
    to_next = remote(atoms_ref.at[pl.ds(80, 48)], before, s_halo.at[0], r_halo.at[0], next_row())
    to_prev = remote(atoms_ref.at[pl.ds(0, 48)], after, s_halo.at[1], r_halo.at[1], prev_row())
    arguments[6].wait()
    ids_next = remote(token_ref, token_before, s_halo.at[2], r_halo.at[2], next_row())
    ids_prev = remote(token_ref, token_after, s_halo.at[3], r_halo.at[3], prev_row())
    to_next.start()
    to_prev.start()
    ids_next.start()
    ids_prev.start()

    plane(lambda group_to, to: remote(send1.at[group_to], recv1.at[group], s_1, r_1, to).start())

    for k in (3, 4, 5, 7, 8, 9):
        arguments[k].wait()
    atoms = atoms_ref[...].astype(F32)
    own = dot(normed(atoms).astype(BF16), w_qkv_ref[...]).astype(BF16)
    line = lax.broadcasted_iota(jnp.int32, (128, 128), 0)
    lane = lax.broadcasted_iota(jnp.int32, (128, 128), 1)
    token_id = 64 * (2 * ((line // 4) % 2) + core) + 4 * (line // 8) + line % 4
    picked = jnp.where(token_id == token_ref[...], 1.0, 0.0).astype(BF16)
    to_next.wait_recv()
    to_prev.wait_recv()
    ids_next.wait_recv()
    ids_prev.wait_recv()
    count = picked.astype(F32)
    for ids in (token_before, token_after):
        count = count + jnp.where(token_id == ids[...], 1.0, 0.0)
    count = jnp.maximum(jnp.sum(count, axis=1, keepdims=True), 1.0)
    edge = jnp.concatenate([before[...], after[...]], axis=0).astype(F32)
    edge = dot(normed(edge).astype(BF16), w_qkv_ref[:, C:]).astype(BF16)
    keys = jnp.concatenate([edge[0:48, :C], own[:, C : 2 * C], edge[48:96, :C]], axis=0)
    values = jnp.concatenate([edge[0:48, C:], own[:, 2 * C :], edge[48:96, C:]], axis=0)
    head_of = lax.broadcasted_iota(jnp.int32, (32, C), 1) // 32
    attended = []
    ones = jnp.ones((128, C), BF16)
    for window in range(4):
        at = 32 * window
        query = own[at : at + 32, :C]
        query = jnp.concatenate(
            [jnp.where(head_of == h, query, jnp.zeros_like(query)) for h in range(HEADS)], axis=0
        )
        scores = dot_nt(query, keys[at : at + 128]) * (32.0**-0.5)
        position = row * 128 + at - 48 + lax.broadcasted_iota(jnp.int32, (128, 128), 1)
        scores = jnp.where((position >= 0) & (position < 8192), scores, -1e30)
        probs = jnp.exp(scores - jnp.max(scores, axis=-1, keepdims=True))
        mixed = dot(probs.astype(BF16), jnp.concatenate([values[at : at + 128], ones], axis=1))
        mixed = mixed[:, :C] / mixed[:, C:]
        result = mixed[0:32]
        for h in range(1, HEADS):
            result = jnp.where(head_of == h, mixed[32 * h : 32 * h + 32], result)
        attended.append(result)
    attended = jnp.concatenate(attended, axis=0).astype(BF16)
    remote(send1.at[pl.ds(0, 31)], recv1.at[pl.ds(0, 31)], s_1, r_1, mate).wait_recv()
    wide[...] = recv1[...].reshape(512, C).astype(F32)
    place = (x // 2) * 2 + core

    def assemble(side, slot):
        for half in range(2):
            at = side * 8 + slot * 2 + half
            even, odd = halves(
                wide[pl.ds(at, 16, stride=16), :], wide[pl.ds(256 + at, 16, stride=16), :]
            )
            both = jnp.concatenate([even, odd], axis=0).astype(BF16)
            if side:
                right[slot, half * 32 : half * 32 + 32, :] = both
            else:
                left[core, slot, half * 32 : half * 32 + 32, :] = both

    def pass_right(part, step):
        return remote(
            right.at[pl.ds(2 * part, 2)], rights.at[place, pl.ds(2 * part, 2)],
            s_2.at[2 * step + part], r_2.at[2 * place + part], along_x(step, parity),
        )

    for part in range(2):
        assemble(1, 2 * part)
        assemble(1, 2 * part + 1)
        for step in (2, 1, 3):
            pass_right(part, step).start()

        @pl.when(jnp.logical_not(own_right))
        def _():
            pass_right(part, 0).start()

    atom_out = (atoms + dot(attended, w_attn_ref[...])).astype(BF16)
    atom_out_ref[...] = atom_out
    hidden = jnp.maximum(dot(atom_out, w_token_ref[...]), 0.0).astype(BF16)
    single = (dot(picked, hidden) / count).astype(BF16)
    k_part = dot(single, w_col_ref[...])
    r_part = dot(single, w_row_ref[...])
    k_swap, r_swap = (pltpu.roll(part.reshape(16, 8, C), 4, 1).reshape(128, C) for part in (k_part, r_part))
    for k_high in range(2):
        for r_high in range(2):
            part = jnp.where(line % 8 < 4, (k_part, k_swap)[k_high], (r_swap, r_part)[r_high])
            tok_send[k_high, r_high] = part.reshape(16, 8, C).astype(BF16)
    tok_recv[pl.ds(row, 1)] = tok_send[pl.ds(z_hi, 1), pl.ds(x // 2, 1), pl.ds(p, 1)].reshape(1, 8, C)

    pl.semaphore_wait(plane_in, 3)

    def give(x_to, piece, to):
        remote(tok_send.at[to[1] // 2, x_to // 2, piece], tok_recv.at[row], s_t, r_t, to).start()

    other_x(give, (2, 7, 1, 0))
    same_x(give, (2, 7, 1, 0))

    @pl.when(own_right)
    def _():
        rights[pl.ds(place, 1)] = right[...][None]

    for slot in range(4):
        assemble(0, slot)
    to_mate = remote(left.at[core], left.at[core], s_l, r_l, mate)
    to_mate.start()

    remote(left.at[1 - core], left.at[1 - core], s_l, r_l, mate).wait_recv()
    for slot in range(4):
        if slot % 2 == 0:
            for source in range(4):

                @pl.when(jnp.logical_not(own_right & (place == source)))
                def _():
                    remote(
                        right.at[pl.ds(slot, 2)], rights.at[source, pl.ds(slot, 2)],
                        s_2.at[0], r_2.at[2 * source + slot // 2], mate,
                    ).wait_recv()

        tri = None
        for k in range(2):
            other = jnp.concatenate([rights[k, slot], rights[2 + k, slot]], axis=0)
            term = dot_nt(left[k, slot], other)
            tri = term if tri is None else tri + term
        for half in range(2):
            first, second = halves(tri[half * 32 : half * 32 + 16], tri[half * 32 + 16 : half * 32 + 32])
            at = slot * 2 + half
            wide[pl.ds(at, 16, stride=8), :] = first
            wide[pl.ds(128 + at, 16, stride=8), :] = second
    send3[...] = wide[0:256, :].reshape(32, 8, C).astype(BF16)
    recv3[pl.ds(group, 1)] = send3[pl.ds(group, 1)]

    plane(lambda group_to, to: remote(send3.at[group_to], recv3.at[group], s_3, r_3, to).start())

    remote(tok_recv.at[pl.ds(0, 63)], tok_recv.at[pl.ds(0, 63)], s_t, r_t, mate).wait_recv()
    k_send[...] = jnp.sum(tok_recv[...].astype(F32), axis=0)
    k_recv[pl.ds(p, 1)] = k_send[...][None]
    for z_step in (3, 2, 1, 0):
        z_to = z_hi * 4 + (z_lo + z_step) % 4
        for step in (2, 1, 3, 0):
            if step or z_step:
                remote(k_send, k_recv.at[p], s_k, r_k, place_of(x, ys[step], z_to)).start()

    @pl.when(own_right)
    def _():
        r_recv[...] = k_send[...]
        remote(k_send, r_recv, s_r, r_r, mate).start()

    remote(send3.at[pl.ds(0, 31)], recv3.at[pl.ds(0, 31)], s_3, r_3, mate).wait_recv()
    wide[0:256, :] = recv3[...].reshape(256, C).astype(F32)
    for half in range(2):
        tri = jnp.concatenate(
            [wide[pl.ds(slot * 2 + half, 32, stride=8), :] for slot in range(4)], axis=0
        )
        centered = tri - jnp.mean(tri, axis=0, keepdims=True)
        variance = jnp.mean(centered * centered, axis=0, keepdims=True)
        tri_norm = (centered * lax.rsqrt(variance + 1e-05)).T.astype(BF16)
        update = dot(tri_norm, tri_out_ref[...])
        for odd in range(2):
            for i in range(4):
                upd_ref[pl.ds((half * 2 + odd) * 64 + i, 16, stride=4), :] = update[
                    odd * 64 + i * 16 : odd * 64 + i * 16 + 16
                ]
    update = pair_ref[...].reshape(256, C).astype(F32) + upd_ref[...] * gate_ref[...]

    remote(k_recv.at[pl.ds(0, 15)], k_recv.at[pl.ds(0, 15)], s_k, r_k, mate).wait_recv()

    @pl.when(jnp.logical_not(own_right))
    def _():
        remote(k_send, r_recv, s_r, r_r, mate).wait_recv()

    k_term = k_recv[...]
    k_term = k_term[:, 0:4].reshape(64, C)
    r_term = r_recv[4:8, :]
    for i in range(4):
        pair_out_ref[i] = (update[i * 64 : i * 64 + 64] + k_term + r_term[i : i + 1]).astype(BF16)

    ids_next.wait_send()
    ids_prev.wait_send()
    to_next.wait_send()
    to_prev.wait_send()
    to_mate.wait_send()
    remote(send1.at[pl.ds(0, 31)], recv1.at[pl.ds(0, 31)], s_1, r_1, mate).wait_send()
    remote(tok_recv.at[pl.ds(0, 63)], tok_recv.at[pl.ds(0, 63)], s_t, r_t, mate).wait_send()
    remote(send3.at[pl.ds(0, 31)], recv3.at[pl.ds(0, 31)], s_3, r_3, mate).wait_send()
    remote(k_recv.at[pl.ds(0, 15)], k_recv.at[pl.ds(0, 15)], s_k, r_k, mate).wait_send()
    for part in range(2):
        for step in range(1, 4):
            pass_right(part, step).wait_send()

        @pl.when(jnp.logical_not(own_right))
        def _():
            pass_right(part, 0).wait_send()

    @pl.when(own_right)
    def _():
        remote(k_send, r_recv, s_r, r_r, mate).wait_send()


def store(pair_in, atoms_in, pair_to, atoms_to, done):
    first = pltpu.make_async_copy(pair_in, pair_to, done.at[0])
    second = pltpu.make_async_copy(atoms_in, atoms_to, done.at[1])
    first.start()
    second.start()
    first.wait()
    second.wait()


def per_device(
    pair, atoms, atom_token, tri_proj, tri_out, w_qkv, w_attn_out, w_token, w_row, w_col
):
    vmem = pl.BlockSpec(memory_space=pltpu.VMEM)
    sem = pltpu.SemaphoreType.DMA
    arguments = (
        pair, atoms, atom_token.reshape(1, 128), tri_proj, tri_out, w_qkv, w_attn_out, w_token,
        w_row, w_col,
    )
    results = pl.pallas_call(
        kernel,
        out_shape=(pltpu.VMEM(pair.shape, BF16), pltpu.VMEM(atoms.shape, BF16)),
        in_specs=[pl.BlockSpec(memory_space=pltpu.HBM)] * 10,
        out_specs=(vmem, vmem),
        scratch_shapes=[
            pltpu.VMEM(pair.shape, BF16),
            pltpu.VMEM(atoms.shape, BF16),
            pltpu.VMEM((1, 128), jnp.int32),
            pltpu.VMEM(tri_proj.shape, BF16),
            pltpu.VMEM(tri_out.shape, BF16),
            pltpu.VMEM(w_qkv.shape, BF16),
            pltpu.VMEM(w_attn_out.shape, BF16),
            pltpu.VMEM(w_token.shape, BF16),
            pltpu.VMEM(w_row.shape, BF16),
            pltpu.VMEM(w_col.shape, BF16),
            pltpu.VMEM((512, C), F32),
            pltpu.VMEM((32, 16, C), BF16),
            pltpu.VMEM((32, 16, C), BF16),
            pltpu.VMEM((2, 4, 64, C), BF16),
            pltpu.VMEM((4, 64, C), BF16),
            pltpu.VMEM((4, 4, 64, C), BF16),
            pltpu.VMEM((32, 8, C), BF16),
            pltpu.VMEM((32, 8, C), BF16),
            pltpu.VMEM((256, C), F32),
            pltpu.VMEM((256, C), F32),
            pltpu.VMEM((48, C), BF16),
            pltpu.VMEM((48, C), BF16),
            pltpu.VMEM((1, 128), jnp.int32),
            pltpu.VMEM((1, 128), jnp.int32),
            pltpu.VMEM((2, 2, 16, 8, C), BF16),
            pltpu.VMEM((64, 8, C), BF16),
            pltpu.VMEM((8, C), F32),
            pltpu.VMEM((16, 8, C), F32),
            pltpu.VMEM((8, C), F32),
            sem((4,)), sem((4,)),
            sem, sem,
            sem((8,)), sem((8,)),
            sem, sem,
            sem, sem,
            sem, sem,
            sem, sem,
            sem, sem,
            sem((10,)),
            pltpu.SemaphoreType.REGULAR,
        ],
        compiler_params=pltpu.CompilerParams(
            collective_id=0, has_side_effects=True, vmem_limit_bytes=32 << 20
        ),
    )(*(pltpu.with_memory_space_constraint(value, pltpu.HBM) for value in arguments))
    hbm = pl.BlockSpec(memory_space=pltpu.HBM)
    return pl.pallas_call(
        store,
        out_shape=(
            jax.ShapeDtypeStruct(pair.shape, BF16),
            jax.ShapeDtypeStruct(atoms.shape, BF16),
        ),
        in_specs=[vmem, vmem],
        out_specs=(hbm, hbm),
        scratch_shapes=[sem((2,))],
    )(*(pltpu.with_memory_space_constraint(value, pltpu.VMEM) for value in results))


def solution(mesh):
    return jax.shard_map(
        per_device,
        mesh=mesh,
        in_specs=(
            P("row", "col", None),
            P("row", None),
            P("row"),
            P(),
            P(),
            P(),
            P(),
            P(),
            P(),
            P(),
        ),
        out_specs=(P("row", "col", None), P("row", None)),
        check_vma=False,
    )
```

```python
import functools

import jax
import jax.numpy as jnp
from jax import lax
from jax.experimental import pallas as pl
from jax.experimental.pallas import tpu as pltpu
from jax.sharding import PartitionSpec as P

MESH = pl.DeviceIdType.MESH
F32 = jnp.float32
BF16 = jnp.bfloat16
HEADS = 4
C = 128


def normed(values):
    mean = jnp.mean(values, axis=-1, keepdims=True)
    centered = values - mean
    variance = jnp.mean(centered * centered, axis=-1, keepdims=True)
    return centered * lax.rsqrt(variance + 1e-05)


def sigmoid(values):
    return 0.5 * jnp.tanh(0.5 * values) + 0.5


def dot(a, b):
    return jnp.dot(a, b, preferred_element_type=F32)


def dot_nt(a, b):
    return lax.dot_general(a, b, (((1,), (1,)), ((), ())), preferred_element_type=F32)


def dot_tn(a, b):
    return lax.dot_general(a, b, (((0,), (0,)), ((), ())), preferred_element_type=F32)


def halves(low, high):
    lane = lax.broadcasted_iota(jnp.int32, low.shape, 1)
    even = jnp.where(lane < 64, low, pltpu.roll(high, 64, 1))
    odd = jnp.where(lane < 64, pltpu.roll(low, 64, 1), high)
    return even, odd


def kernel(
    pair_in, atoms_in, token_in, tri_proj_in, tri_out_in, w_qkv_in, w_attn_in, w_token_in, w_row_in,
    w_col_in, pair_out_ref, atom_out_ref,
    pair_ref, atoms_ref, token_ref, tri_proj_ref, tri_out_ref, w_qkv_ref, w_attn_ref, w_token_ref,
    w_row_ref, w_col_ref,
    wide, send1, recv1, left, right, rights, send3, recv3, gate_ref, upd_ref,
    before, after, token_before, token_after, tok_send, tok_recv, k_send, k_recv, r_recv,
    s_halo, r_halo, s_1, r_1, s_2, r_2, s_l, r_l, s_3, r_3, s_t, r_t, s_k, r_k, s_r, r_r,
    s_in, plane_in,
):
    row, col = lax.axis_index("row"), lax.axis_index("col")
    x, p = row // 16, row % 16
    y, z_lo = p // 4, p % 4
    z_hi, core = col // 2, col % 2
    z = z_hi * 4 + z_lo
    group = z_hi * 16 + p
    parity = x % 2

    ys = [(y + step) % 4 for step in range(4)]

    def place_of(x_to, y_to, z_to):
        return (x_to * 16 + y_to * 4 + z_to % 4, 2 * (z_to // 4) + core)

    def plane(act):
        @pl.loop(0, 7)
        def _(k):
            z_to = (z + 4 + ((k + 1) // 2) * (1 - 2 * (k % 2))) % 8
            for step in (2, 1, 3, 0):
                act((z_to // 4) * 16 + ys[step] * 4 + z_to % 4, place_of(x, ys[step], z_to))

        for step in (2, 1, 3):
            act(z_hi * 16 + ys[step] * 4 + z_lo, place_of(x, ys[step], z))

    def other_x(act, z_steps):
        @pl.loop(0, 3)
        def _(k):
            x_to = (x + 2 + ((k + 1) // 2) * (1 - 2 * (k % 2))) % 4
            for z_step in z_steps:
                z_to = (z + z_step) % 8
                for step in (2, 1, 3, 0):
                    act(x_to, ys[step] * 4 + z_to % 4, place_of(x_to, ys[step], z_to))

    def same_x(act, z_steps):
        for z_step in z_steps:
            z_to = (z + z_step) % 8
            for step in (2, 1, 3, 0):
                if step or z_step:
                    act(x, ys[step] * 4 + z_to % 4, place_of(x, ys[step], z_to))

    def next_row():
        carry_y = (z_lo + 1) // 4
        carry_x = (y + carry_y) // 4
        z_to = (z + 1) % 8
        row_to = ((x + carry_x) % 4) * 16 + ((y + carry_y) % 4) * 4 + z_to % 4
        return (row_to, 2 * (z_to // 4) + core)

    def prev_row():
        carry_y = (4 - z_lo) // 4
        carry_x = (3 - y + carry_y) // 4
        z_to = (z + 7) % 8
        row_to = ((x + 4 - carry_x) % 4) * 16 + ((y + 4 - carry_y) % 4) * 4 + z_to % 4
        return (row_to, 2 * (z_to // 4) + core)

    def along_x(step, core_to):
        return (((x + step) % 4) * 16 + p, 2 * z_hi + core_to)

    mate = (row, 2 * z_hi + 1 - core)
    own_right = parity == core

    def remote(src, dst, send_sem, recv_sem, to):
        return pltpu.make_async_remote_copy(
            src_ref=src, dst_ref=dst, send_sem=send_sem, recv_sem=recv_sem, device_id=to, device_id_type=MESH
        )

    arguments = [
        pltpu.make_async_copy(source, target, s_in.at[k])
        for k, (source, target) in enumerate(
            (
                (pair_in, pair_ref),
                (tri_proj_in, tri_proj_ref),
                (atoms_in, atoms_ref),
                (w_qkv_in, w_qkv_ref),
                (w_attn_in, w_attn_ref),
                (w_token_in, w_token_ref),
                (token_in, token_ref),
                (tri_out_in, tri_out_ref),
                (w_row_in, w_row_ref),
                (w_col_in, w_col_ref),
            )
        )
    ]

    barrier = pltpu.get_barrier_semaphore()

    def hello(to):
        pl.semaphore_signal(barrier, inc=1, device_id=to, device_id_type=MESH)

    plane(lambda group_to, to: hello(to))
    for step in (2, 1, 3):
        hello(along_x(step, core))
        hello(along_x(step, 1 - core))
    hello(next_row())
    hello(prev_row())
    hello(mate)

    for k in range(10):
        arguments[k].start()

    arguments[0].wait()
    arguments[1].wait()
    pair_norm = normed(pair_ref[...].reshape(256, C).astype(F32)).astype(BF16)
    for side in range(2):
        at = 2 * side * C
        gated = sigmoid(dot(pair_norm, tri_proj_ref[:, at : at + C])) * dot(
            pair_norm, tri_proj_ref[:, at + C : at + 2 * C]
        )
        for half in range(2):
            flat = gated[half * 128 : half * 128 + 128].T
            for slot in range(4):
                wide[pl.ds(side * 8 + slot * 2 + half, 32, stride=16), :] = flat[slot * 32 : slot * 32 + 32]
    send1[...] = wide[...].reshape(32, 16, C).astype(BF16)
    recv1[pl.ds(group, 1)] = send1[pl.ds(group, 1)]
    gate_ref[...] = sigmoid(dot(pair_norm, tri_proj_ref[:, 4 * C :]))

    pl.semaphore_wait(barrier, 31 + 6 + 2 + 1)
    for step in (2, 1, 3):
        pl.semaphore_signal(plane_in, inc=1, device_id=along_x(step, core), device_id_type=MESH)

    arguments[2].wait()
    to_next = remote(atoms_ref.at[pl.ds(80, 48)], before, s_halo.at[0], r_halo.at[0], next_row())
    to_prev = remote(atoms_ref.at[pl.ds(0, 48)], after, s_halo.at[1], r_halo.at[1], prev_row())
    arguments[6].wait()
    ids_next = remote(token_ref, token_before, s_halo.at[2], r_halo.at[2], next_row())
    ids_prev = remote(token_ref, token_after, s_halo.at[3], r_halo.at[3], prev_row())
    to_next.start()
    to_prev.start()
    ids_next.start()
    ids_prev.start()

    plane(lambda group_to, to: remote(send1.at[group_to], recv1.at[group], s_1, r_1, to).start())

    for k in (3, 4, 5, 7, 8, 9):
        arguments[k].wait()
    atoms = atoms_ref[...].astype(F32)
    own = dot(normed(atoms).astype(BF16), w_qkv_ref[...]).astype(BF16)
    line = lax.broadcasted_iota(jnp.int32, (128, 128), 0)
    lane = lax.broadcasted_iota(jnp.int32, (128, 128), 1)
    token_id = 64 * (2 * ((line // 4) % 2) + core) + 4 * (line // 8) + line % 4
    picked = jnp.where(token_id == token_ref[...], 1.0, 0.0).astype(BF16)
    to_next.wait_recv()
    to_prev.wait_recv()
    ids_next.wait_recv()
    ids_prev.wait_recv()
    count = picked.astype(F32)
    for ids in (token_before, token_after):
        count = count + jnp.where(token_id == ids[...], 1.0, 0.0)
    count = jnp.maximum(jnp.sum(count, axis=1, keepdims=True), 1.0)
    edge = jnp.concatenate([before[...], after[...]], axis=0).astype(F32)
    edge = dot(normed(edge).astype(BF16), w_qkv_ref[:, C:]).astype(BF16)
    keys = jnp.concatenate([edge[0:48, :C], own[:, C : 2 * C], edge[48:96, :C]], axis=0)
    values = jnp.concatenate([edge[0:48, C:], own[:, 2 * C :], edge[48:96, C:]], axis=0)
    head_of = lax.broadcasted_iota(jnp.int32, (32, C), 1) // 32
    attended = []
    ones = jnp.ones((128, C), BF16)
    for window in range(4):
        at = 32 * window
        query = own[at : at + 32, :C]
        query = jnp.concatenate(
            [jnp.where(head_of == h, query, jnp.zeros_like(query)) for h in range(HEADS)], axis=0
        )
        scores = dot_nt(keys[at : at + 128], query) * (32.0**-0.5)
        position = row * 128 + at - 48 + line
        scores = jnp.where((position >= 0) & (position < 8192), scores, -1e30)
        probs = jnp.exp(scores - jnp.max(scores, axis=0, keepdims=True))
        mixed = dot_tn(probs.astype(BF16), jnp.concatenate([values[at : at + 128], ones], axis=1))
        mixed = mixed[:, :C] / mixed[:, C:]
        result = mixed[0:32]
        for h in range(1, HEADS):
            result = jnp.where(head_of == h, mixed[32 * h : 32 * h + 32], result)
        attended.append(result)
    attended = jnp.concatenate(attended, axis=0).astype(BF16)
    remote(send1.at[pl.ds(0, 31)], recv1.at[pl.ds(0, 31)], s_1, r_1, mate).wait_recv()
    wide[...] = recv1[...].reshape(512, C).astype(F32)
    place = (x // 2) * 2 + core

    def assemble(side, slot):
        for half in range(2):
            at = side * 8 + slot * 2 + half
            even, odd = halves(
                wide[pl.ds(at, 16, stride=16), :], wide[pl.ds(256 + at, 16, stride=16), :]
            )
            both = jnp.concatenate([even, odd], axis=0).astype(BF16)
            if side:
                right[slot, half * 32 : half * 32 + 32, :] = both
            else:
                left[core, slot, half * 32 : half * 32 + 32, :] = both

    def pass_right(part, step):
        return remote(
            right.at[part], rights.at[place, part],
            s_2.at[4 * step + part], r_2.at[4 * place + part], along_x(step, parity),
        )

    for part in range(4):
        assemble(1, part)
        for step in (2, 1, 3):
            pass_right(part, step).start()

        @pl.when(jnp.logical_not(own_right))
        def _():
            pass_right(part, 0).start()

    atom_out = (atoms + dot(attended, w_attn_ref[...])).astype(BF16)
    atom_out_ref[...] = atom_out
    hidden = jnp.maximum(dot(atom_out, w_token_ref[...]), 0.0).astype(BF16)
    single = (dot(picked, hidden) / count).astype(BF16)
    k_part = dot(single, w_col_ref[...])
    r_part = dot(single, w_row_ref[...])
    k_swap, r_swap = (pltpu.roll(part.reshape(16, 8, C), 4, 1).reshape(128, C) for part in (k_part, r_part))
    for k_high in range(2):
        for r_high in range(2):
            part = jnp.where(line % 8 < 4, (k_part, k_swap)[k_high], (r_swap, r_part)[r_high])
            tok_send[k_high, r_high] = part.reshape(16, 8, C).astype(BF16)
    tok_recv[pl.ds(row, 1)] = tok_send[pl.ds(z_hi, 1), pl.ds(x // 2, 1), pl.ds(p, 1)].reshape(1, 8, C)

    pl.semaphore_wait(plane_in, 3)

    def give(x_to, piece, to):
        remote(tok_send.at[to[1] // 2, x_to // 2, piece], tok_recv.at[row], s_t, r_t, to).start()

    other_x(give, (2, 7, 1, 0))
    same_x(give, (2, 7, 1, 0))

    @pl.when(own_right)
    def _():
        rights[pl.ds(place, 1)] = right[...][None]

    for slot in range(4):
        assemble(0, slot)
    to_mate = remote(left.at[core], left.at[core], s_l, r_l, mate)
    to_mate.start()

    remote(left.at[1 - core], left.at[1 - core], s_l, r_l, mate).wait_recv()
    for slot in range(4):
        for source in range(4):

            @pl.when(jnp.logical_not(own_right & (place == source)))
            def _():
                remote(
                    right.at[slot], rights.at[source, slot], s_2.at[0], r_2.at[4 * source + slot], mate
                ).wait_recv()

        tri = None
        for k in range(2):
            other = jnp.concatenate([rights[k, slot], rights[2 + k, slot]], axis=0)
            term = dot_nt(left[k, slot], other)
            tri = term if tri is None else tri + term
        for half in range(2):
            first, second = halves(tri[half * 32 : half * 32 + 16], tri[half * 32 + 16 : half * 32 + 32])
            at = slot * 2 + half
            wide[pl.ds(at, 16, stride=8), :] = first
            wide[pl.ds(128 + at, 16, stride=8), :] = second
    send3[...] = wide[0:256, :].reshape(32, 8, C).astype(BF16)
    recv3[pl.ds(group, 1)] = send3[pl.ds(group, 1)]

    plane(lambda group_to, to: remote(send3.at[group_to], recv3.at[group], s_3, r_3, to).start())

    remote(tok_recv.at[pl.ds(0, 63)], tok_recv.at[pl.ds(0, 63)], s_t, r_t, mate).wait_recv()
    k_send[...] = jnp.sum(tok_recv[...].astype(F32), axis=0).astype(BF16)
    k_recv[pl.ds(p, 1)] = k_send[...][None]
    for z_step in (3, 2, 1, 0):
        z_to = z_hi * 4 + (z_lo + z_step) % 4
        for step in (2, 1, 3, 0):
            if step or z_step:
                remote(k_send, k_recv.at[p], s_k, r_k, place_of(x, ys[step], z_to)).start()

    @pl.when(own_right)
    def _():
        r_recv[...] = k_send[...]
        remote(k_send, r_recv, s_r, r_r, mate).start()

    remote(send3.at[pl.ds(0, 31)], recv3.at[pl.ds(0, 31)], s_3, r_3, mate).wait_recv()
    wide[0:256, :] = recv3[...].reshape(256, C).astype(F32)
    for half in range(2):
        tri = jnp.concatenate(
            [wide[pl.ds(slot * 2 + half, 32, stride=8), :] for slot in range(4)], axis=0
        )
        centered = tri - jnp.mean(tri, axis=0, keepdims=True)
        variance = jnp.mean(centered * centered, axis=0, keepdims=True)
        tri_norm = (centered * lax.rsqrt(variance + 1e-05)).T.astype(BF16)
        update = dot(tri_norm, tri_out_ref[...])
        for odd in range(2):
            for i in range(4):
                upd_ref[pl.ds((half * 2 + odd) * 64 + i, 16, stride=4), :] = update[
                    odd * 64 + i * 16 : odd * 64 + i * 16 + 16
                ]
    update = pair_ref[...].reshape(256, C).astype(F32) + upd_ref[...] * gate_ref[...]

    remote(k_recv.at[pl.ds(0, 15)], k_recv.at[pl.ds(0, 15)], s_k, r_k, mate).wait_recv()

    @pl.when(jnp.logical_not(own_right))
    def _():
        remote(k_send, r_recv, s_r, r_r, mate).wait_recv()

    k_term = k_recv[...].astype(F32)
    k_term = k_term[:, 0:4].reshape(64, C)
    r_term = r_recv[...].astype(F32)[4:8]
    for i in range(4):
        pair_out_ref[i] = (update[i * 64 : i * 64 + 64] + k_term + r_term[i : i + 1]).astype(BF16)

    ids_next.wait_send()
    ids_prev.wait_send()
    to_next.wait_send()
    to_prev.wait_send()
    to_mate.wait_send()
    remote(send1.at[pl.ds(0, 31)], recv1.at[pl.ds(0, 31)], s_1, r_1, mate).wait_send()
    remote(tok_recv.at[pl.ds(0, 63)], tok_recv.at[pl.ds(0, 63)], s_t, r_t, mate).wait_send()
    remote(send3.at[pl.ds(0, 31)], recv3.at[pl.ds(0, 31)], s_3, r_3, mate).wait_send()
    remote(k_recv.at[pl.ds(0, 15)], k_recv.at[pl.ds(0, 15)], s_k, r_k, mate).wait_send()
    for part in range(4):
        for step in range(1, 4):
            pass_right(part, step).wait_send()

        @pl.when(jnp.logical_not(own_right))
        def _():
            pass_right(part, 0).wait_send()

    @pl.when(own_right)
    def _():
        remote(k_send, r_recv, s_r, r_r, mate).wait_send()


def store(pair_in, atoms_in, pair_to, atoms_to, done):
    first = pltpu.make_async_copy(pair_in, pair_to, done.at[0])
    second = pltpu.make_async_copy(atoms_in, atoms_to, done.at[1])
    first.start()
    second.start()
    first.wait()
    second.wait()


def per_device(
    pair, atoms, atom_token, tri_proj, tri_out, w_qkv, w_attn_out, w_token, w_row, w_col
):
    vmem = pl.BlockSpec(memory_space=pltpu.VMEM)
    sem = pltpu.SemaphoreType.DMA
    arguments = (
        pair, atoms, atom_token.reshape(1, 128), tri_proj, tri_out, w_qkv, w_attn_out, w_token,
        w_row, w_col,
    )
    results = pl.pallas_call(
        kernel,
        out_shape=(pltpu.VMEM(pair.shape, BF16), pltpu.VMEM(atoms.shape, BF16)),
        in_specs=[pl.BlockSpec(memory_space=pltpu.HBM)] * 10,
        out_specs=(vmem, vmem),
        scratch_shapes=[
            pltpu.VMEM(pair.shape, BF16),
            pltpu.VMEM(atoms.shape, BF16),
            pltpu.VMEM((1, 128), jnp.int32),
            pltpu.VMEM(tri_proj.shape, BF16),
            pltpu.VMEM(tri_out.shape, BF16),
            pltpu.VMEM(w_qkv.shape, BF16),
            pltpu.VMEM(w_attn_out.shape, BF16),
            pltpu.VMEM(w_token.shape, BF16),
            pltpu.VMEM(w_row.shape, BF16),
            pltpu.VMEM(w_col.shape, BF16),
            pltpu.VMEM((512, C), F32),
            pltpu.VMEM((32, 16, C), BF16),
            pltpu.VMEM((32, 16, C), BF16),
            pltpu.VMEM((2, 4, 64, C), BF16),
            pltpu.VMEM((4, 64, C), BF16),
            pltpu.VMEM((4, 4, 64, C), BF16),
            pltpu.VMEM((32, 8, C), BF16),
            pltpu.VMEM((32, 8, C), BF16),
            pltpu.VMEM((256, C), F32),
            pltpu.VMEM((256, C), F32),
            pltpu.VMEM((48, C), BF16),
            pltpu.VMEM((48, C), BF16),
            pltpu.VMEM((1, 128), jnp.int32),
            pltpu.VMEM((1, 128), jnp.int32),
            pltpu.VMEM((2, 2, 16, 8, C), BF16),
            pltpu.VMEM((64, 8, C), BF16),
            pltpu.VMEM((8, C), BF16),
            pltpu.VMEM((16, 8, C), BF16),
            pltpu.VMEM((8, C), BF16),
            sem((4,)), sem((4,)),
            sem, sem,
            sem((16,)), sem((16,)),
            sem, sem,
            sem, sem,
            sem, sem,
            sem, sem,
            sem, sem,
            sem((10,)),
            pltpu.SemaphoreType.REGULAR,
        ],
        compiler_params=pltpu.CompilerParams(
            collective_id=0, has_side_effects=True, vmem_limit_bytes=32 << 20
        ),
    )(*(pltpu.with_memory_space_constraint(value, pltpu.HBM) for value in arguments))
    hbm = pl.BlockSpec(memory_space=pltpu.HBM)
    return pl.pallas_call(
        store,
        out_shape=(
            jax.ShapeDtypeStruct(pair.shape, BF16),
            jax.ShapeDtypeStruct(atoms.shape, BF16),
        ),
        in_specs=[vmem, vmem],
        out_specs=(hbm, hbm),
        scratch_shapes=[sem((2,))],
    )(*(pltpu.with_memory_space_constraint(value, pltpu.VMEM) for value in results))


def solution(mesh):
    return jax.shard_map(
        per_device,
        mesh=mesh,
        in_specs=(
            P("row", "col", None),
            P("row", None),
            P("row"),
            P(),
            P(),
            P(),
            P(),
            P(),
            P(),
            P(),
        ),
        out_specs=(P("row", "col", None), P("row", None)),
        check_vma=False,
    )
```

```python
import functools

import jax
import jax.numpy as jnp
from jax import lax
from jax.experimental import pallas as pl
from jax.experimental.pallas import tpu as pltpu
from jax.sharding import PartitionSpec as P

MESH = pl.DeviceIdType.MESH
F32 = jnp.float32
BF16 = jnp.bfloat16
HEADS = 4
C = 128


def normed(values):
    mean = jnp.mean(values, axis=-1, keepdims=True)
    centered = values - mean
    variance = jnp.mean(centered * centered, axis=-1, keepdims=True)
    return centered * lax.rsqrt(variance + 1e-05)


def sigmoid(values):
    return 0.5 * jnp.tanh(0.5 * values) + 0.5


def dot(a, b):
    return jnp.dot(a, b, preferred_element_type=F32)


def dot_nt(a, b):
    return lax.dot_general(a, b, (((1,), (1,)), ((), ())), preferred_element_type=F32)


def dot_tn(a, b):
    return lax.dot_general(a, b, (((0,), (0,)), ((), ())), preferred_element_type=F32)


def halves(low, high):
    lane = lax.broadcasted_iota(jnp.int32, low.shape, 1)
    even = jnp.where(lane < 64, low, pltpu.roll(high, 64, 1))
    odd = jnp.where(lane < 64, pltpu.roll(low, 64, 1), high)
    return even, odd


def kernel(
    pair_in, atoms_in, token_in, tri_proj_in, tri_out_in, w_qkv_in, w_attn_in, w_token_in, w_row_in,
    w_col_in, pair_out_ref, atom_out_ref,
    pair_ref, atoms_ref, token_ref, tri_proj_ref, tri_out_ref, w_qkv_ref, w_attn_ref, w_token_ref,
    w_row_ref, w_col_ref,
    wide, send1, recv1, left, right, rights, send3, recv3, gate_ref, upd_ref,
    before, after, token_before, token_after, tok_send, tok_recv, k_send, k_recv, r_recv,
    s_halo, r_halo, s_1, r_1, s_2, r_2, s_l, r_l, s_3, r_3, s_t, r_t, s_k, r_k, s_r, r_r,
    s_in, plane_in,
):
    row, col = lax.axis_index("row"), lax.axis_index("col")
    x, p = row // 16, row % 16
    y, z_lo = p // 4, p % 4
    z_hi, core = col // 2, col % 2
    z = z_hi * 4 + z_lo
    group = z_hi * 16 + p
    parity = x % 2

    ys = [(y + step) % 4 for step in range(4)]

    def place_of(x_to, y_to, z_to):
        return (x_to * 16 + y_to * 4 + z_to % 4, 2 * (z_to // 4) + core)

    def plane(act):
        @pl.loop(0, 7)
        def _(k):
            z_to = (z + 4 + ((k + 1) // 2) * (1 - 2 * (k % 2))) % 8
            for step in (2, 1, 3, 0):
                act((z_to // 4) * 16 + ys[step] * 4 + z_to % 4, place_of(x, ys[step], z_to))

        for step in (2, 1, 3):
            act(z_hi * 16 + ys[step] * 4 + z_lo, place_of(x, ys[step], z))

    def other_x(act, z_steps):
        @pl.loop(0, 3)
        def _(k):
            x_to = (x + 2 + ((k + 1) // 2) * (1 - 2 * (k % 2))) % 4
            for z_step in z_steps:
                z_to = (z + z_step) % 8
                for step in (2, 1, 3, 0):
                    act(x_to, ys[step] * 4 + z_to % 4, place_of(x_to, ys[step], z_to))

    def same_x(act, z_steps):
        for z_step in z_steps:
            z_to = (z + z_step) % 8
            for step in (2, 1, 3, 0):
                if step or z_step:
                    act(x, ys[step] * 4 + z_to % 4, place_of(x, ys[step], z_to))

    def next_row():
        carry_y = (z_lo + 1) // 4
        carry_x = (y + carry_y) // 4
        z_to = (z + 1) % 8
        row_to = ((x + carry_x) % 4) * 16 + ((y + carry_y) % 4) * 4 + z_to % 4
        return (row_to, 2 * (z_to // 4) + core)

    def prev_row():
        carry_y = (4 - z_lo) // 4
        carry_x = (3 - y + carry_y) // 4
        z_to = (z + 7) % 8
        row_to = ((x + 4 - carry_x) % 4) * 16 + ((y + 4 - carry_y) % 4) * 4 + z_to % 4
        return (row_to, 2 * (z_to // 4) + core)

    def along_x(step, core_to):
        return (((x + step) % 4) * 16 + p, 2 * z_hi + core_to)

    mate = (row, 2 * z_hi + 1 - core)
    own_right = parity == core

    def remote(src, dst, send_sem, recv_sem, to):
        return pltpu.make_async_remote_copy(
            src_ref=src, dst_ref=dst, send_sem=send_sem, recv_sem=recv_sem, device_id=to, device_id_type=MESH
        )

    arguments = [
        pltpu.make_async_copy(source, target, s_in.at[k])
        for k, (source, target) in enumerate(
            (
                (pair_in, pair_ref),
                (tri_proj_in, tri_proj_ref),
                (atoms_in, atoms_ref),
                (w_qkv_in, w_qkv_ref),
                (w_attn_in, w_attn_ref),
                (w_token_in, w_token_ref),
                (token_in, token_ref),
                (tri_out_in, tri_out_ref),
                (w_row_in, w_row_ref),
                (w_col_in, w_col_ref),
            )
        )
    ]

    barrier = pltpu.get_barrier_semaphore()

    def hello(to):
        pl.semaphore_signal(barrier, inc=1, device_id=to, device_id_type=MESH)

    plane(lambda group_to, to: hello(to))
    for step in (2, 1, 3):
        hello(along_x(step, core))
        hello(along_x(step, 1 - core))
    hello(next_row())
    hello(prev_row())
    hello(mate)

    for k in range(10):
        arguments[k].start()

    arguments[0].wait()
    arguments[1].wait()
    pair_norm = normed(pair_ref[...].reshape(256, C).astype(F32)).astype(BF16)
    for side in range(2):
        at = 2 * side * C
        gated = sigmoid(dot(pair_norm, tri_proj_ref[:, at : at + C])) * dot(
            pair_norm, tri_proj_ref[:, at + C : at + 2 * C]
        )
        for half in range(2):
            flat = gated[half * 128 : half * 128 + 128].T
            for slot in range(4):
                wide[pl.ds(side * 8 + slot * 2 + half, 32, stride=16), :] = flat[slot * 32 : slot * 32 + 32]
    send1[...] = wide[...].reshape(32, 16, C).astype(BF16)
    recv1[pl.ds(group, 1)] = send1[pl.ds(group, 1)]
    gate_ref[...] = sigmoid(dot(pair_norm, tri_proj_ref[:, 4 * C :]))

    pl.semaphore_wait(barrier, 31 + 6 + 2 + 1)
    for step in (2, 1, 3):
        pl.semaphore_signal(plane_in, inc=1, device_id=along_x(step, core), device_id_type=MESH)

    arguments[2].wait()
    to_next = remote(atoms_ref.at[pl.ds(80, 48)], before, s_halo.at[0], r_halo.at[0], next_row())
    to_prev = remote(atoms_ref.at[pl.ds(0, 48)], after, s_halo.at[1], r_halo.at[1], prev_row())
    arguments[6].wait()
    ids_next = remote(token_ref, token_before, s_halo.at[2], r_halo.at[2], next_row())
    ids_prev = remote(token_ref, token_after, s_halo.at[3], r_halo.at[3], prev_row())
    to_next.start()
    to_prev.start()
    ids_next.start()
    ids_prev.start()

    plane(lambda group_to, to: remote(send1.at[group_to], recv1.at[group], s_1, r_1, to).start())

    for k in (3, 4, 5, 7, 8, 9):
        arguments[k].wait()
    atoms = atoms_ref[...].astype(F32)
    own = dot(normed(atoms).astype(BF16), w_qkv_ref[...]).astype(BF16)
    line = lax.broadcasted_iota(jnp.int32, (128, 128), 0)
    lane = lax.broadcasted_iota(jnp.int32, (128, 128), 1)
    token_id = 64 * (2 * ((line // 4) % 2) + core) + 4 * (line // 8) + line % 4
    picked = jnp.where(token_id == token_ref[...], 1.0, 0.0).astype(BF16)
    to_next.wait_recv()
    to_prev.wait_recv()
    ids_next.wait_recv()
    ids_prev.wait_recv()
    count = picked.astype(F32)
    for ids in (token_before, token_after):
        count = count + jnp.where(token_id == ids[...], 1.0, 0.0)
    count = jnp.maximum(jnp.sum(count, axis=1, keepdims=True), 1.0)
    edge = jnp.concatenate([before[...], after[...]], axis=0).astype(F32)
    edge = dot(normed(edge).astype(BF16), w_qkv_ref[:, C:]).astype(BF16)
    keys = jnp.concatenate([edge[0:48, :C], own[:, C : 2 * C], edge[48:96, :C]], axis=0)
    values = jnp.concatenate([edge[0:48, C:], own[:, 2 * C :], edge[48:96, C:]], axis=0)
    head_of = lax.broadcasted_iota(jnp.int32, (32, C), 1) // 32
    attended = []
    ones = jnp.ones((128, C), BF16)
    for window in range(4):
        at = 32 * window
        query = own[at : at + 32, :C]
        query = jnp.concatenate(
            [jnp.where(head_of == h, query, jnp.zeros_like(query)) for h in range(HEADS)], axis=0
        )
        scores = dot_nt(keys[at : at + 128], query) * (32.0**-0.5)
        position = row * 128 + at - 48 + line
        scores = jnp.where((position >= 0) & (position < 8192), scores, -1e30)
        probs = jnp.exp(scores - jnp.max(scores, axis=0, keepdims=True))
        mixed = dot_tn(probs.astype(BF16), jnp.concatenate([values[at : at + 128], ones], axis=1))
        mixed = mixed[:, :C] / mixed[:, C:]
        result = mixed[0:32]
        for h in range(1, HEADS):
            result = jnp.where(head_of == h, mixed[32 * h : 32 * h + 32], result)
        attended.append(result)
    attended = jnp.concatenate(attended, axis=0).astype(BF16)
    remote(send1.at[pl.ds(0, 31)], recv1.at[pl.ds(0, 31)], s_1, r_1, mate).wait_recv()
    wide[...] = recv1[...].reshape(512, C).astype(F32)
    place = (x // 2) * 2 + core

    def assemble(side, slot):
        for half in range(2):
            at = side * 8 + slot * 2 + half
            even, odd = halves(
                wide[pl.ds(at, 16, stride=16), :], wide[pl.ds(256 + at, 16, stride=16), :]
            )
            both = jnp.concatenate([even, odd], axis=0).astype(BF16)
            if side:
                right[slot, half * 32 : half * 32 + 32, :] = both
            else:
                left[core, slot, half * 32 : half * 32 + 32, :] = both

    def pass_right(part, step):
        return remote(
            right.at[part], rights.at[place, part],
            s_2.at[4 * step + part], r_2.at[4 * place + part], along_x(step, parity),
        )

    for part in range(4):
        assemble(1, part)
        for step in (2, 1, 3):
            pass_right(part, step).start()

        @pl.when(jnp.logical_not(own_right))
        def _():
            pass_right(part, 0).start()

    atom_out = (atoms + dot(attended, w_attn_ref[...])).astype(BF16)
    atom_out_ref[...] = atom_out
    hidden = jnp.maximum(dot(atom_out, w_token_ref[...]), 0.0).astype(BF16)
    single = (dot(picked, hidden) / count).astype(BF16)
    k_part = dot(single, w_col_ref[...])
    r_part = dot(single, w_row_ref[...])
    k_swap, r_swap = (pltpu.roll(part.reshape(16, 8, C), 4, 1).reshape(128, C) for part in (k_part, r_part))
    for k_high in range(2):
        for r_high in range(2):
            part = jnp.where(line % 8 < 4, (k_part, k_swap)[k_high], (r_swap, r_part)[r_high])
            tok_send[k_high, r_high] = part.reshape(16, 8, C).astype(BF16)
    tok_recv[pl.ds(row, 1)] = tok_send[pl.ds(z_hi, 1), pl.ds(x // 2, 1), pl.ds(p, 1)].reshape(1, 8, C)

    pl.semaphore_wait(plane_in, 3)

    def give(x_to, piece, to):
        remote(tok_send.at[to[1] // 2, x_to // 2, piece], tok_recv.at[row], s_t, r_t, to).start()

    other_x(give, (2, 7, 1, 0))
    same_x(give, (2, 7, 1, 0))

    @pl.when(own_right)
    def _():
        rights[pl.ds(place, 1)] = right[...][None]

    for slot in range(4):
        assemble(0, slot)
    to_mate = remote(left.at[core], left.at[core], s_l, r_l, mate)
    to_mate.start()

    remote(left.at[1 - core], left.at[1 - core], s_l, r_l, mate).wait_recv()
    for slot in range(4):
        for source in range(4):

            @pl.when(jnp.logical_not(own_right & (place == source)))
            def _():
                remote(
                    right.at[slot], rights.at[source, slot], s_2.at[0], r_2.at[4 * source + slot], mate
                ).wait_recv()

        tri = None
        for k in range(2):
            other = jnp.concatenate([rights[k, slot], rights[2 + k, slot]], axis=0)
            term = dot_nt(left[k, slot], other)
            tri = term if tri is None else tri + term
        for half in range(2):
            first, second = halves(tri[half * 32 : half * 32 + 16], tri[half * 32 + 16 : half * 32 + 32])
            at = slot * 2 + half
            wide[pl.ds(at, 16, stride=8), :] = first
            wide[pl.ds(128 + at, 16, stride=8), :] = second
    send3[...] = wide[0:256, :].reshape(32, 8, C).astype(BF16)
    recv3[pl.ds(group, 1)] = send3[pl.ds(group, 1)]

    plane(lambda group_to, to: remote(send3.at[group_to], recv3.at[group], s_3, r_3, to).start())

    remote(tok_recv.at[pl.ds(0, 63)], tok_recv.at[pl.ds(0, 63)], s_t, r_t, mate).wait_recv()
    k_send[...] = jnp.sum(tok_recv[...].astype(F32), axis=0).astype(BF16)
    k_recv[pl.ds(p, 1)] = k_send[...][None]
    for z_step in (3, 2, 1, 0):
        z_to = z_hi * 4 + (z_lo + z_step) % 4
        for step in (2, 1, 3, 0):
            if step or z_step:
                remote(k_send, k_recv.at[p], s_k, r_k, place_of(x, ys[step], z_to)).start()

    @pl.when(own_right)
    def _():
        r_recv[...] = k_send[...]
        remote(k_send, r_recv, s_r, r_r, mate).start()

    remote(send3.at[pl.ds(0, 31)], recv3.at[pl.ds(0, 31)], s_3, r_3, mate).wait_recv()
    wide[0:256, :] = recv3[...].reshape(256, C).astype(F32)
    for half in range(2):
        tri = jnp.concatenate(
            [wide[pl.ds(slot * 2 + half, 32, stride=8), :] for slot in range(4)], axis=0
        )
        centered = tri - jnp.mean(tri, axis=0, keepdims=True)
        variance = jnp.mean(centered * centered, axis=0, keepdims=True)
        tri_norm = (centered * lax.rsqrt(variance + 1e-05)).astype(BF16)
        update = dot_tn(tri_norm, tri_out_ref[...])
        for odd in range(2):
            for i in range(4):
                upd_ref[pl.ds((half * 2 + odd) * 64 + i, 16, stride=4), :] = update[
                    odd * 64 + i * 16 : odd * 64 + i * 16 + 16
                ]
    update = pair_ref[...].reshape(256, C).astype(F32) + upd_ref[...] * gate_ref[...]

    remote(k_recv.at[pl.ds(0, 15)], k_recv.at[pl.ds(0, 15)], s_k, r_k, mate).wait_recv()

    @pl.when(jnp.logical_not(own_right))
    def _():
        remote(k_send, r_recv, s_r, r_r, mate).wait_recv()

    k_term = k_recv[...].astype(F32)
    k_term = k_term[:, 0:4].reshape(64, C)
    r_term = r_recv[...].astype(F32)[4:8]
    for i in range(4):
        pair_out_ref[i] = (update[i * 64 : i * 64 + 64] + k_term + r_term[i : i + 1]).astype(BF16)

    ids_next.wait_send()
    ids_prev.wait_send()
    to_next.wait_send()
    to_prev.wait_send()
    to_mate.wait_send()
    remote(send1.at[pl.ds(0, 31)], recv1.at[pl.ds(0, 31)], s_1, r_1, mate).wait_send()
    remote(tok_recv.at[pl.ds(0, 63)], tok_recv.at[pl.ds(0, 63)], s_t, r_t, mate).wait_send()
    remote(send3.at[pl.ds(0, 31)], recv3.at[pl.ds(0, 31)], s_3, r_3, mate).wait_send()
    remote(k_recv.at[pl.ds(0, 15)], k_recv.at[pl.ds(0, 15)], s_k, r_k, mate).wait_send()
    for part in range(4):
        for step in range(1, 4):
            pass_right(part, step).wait_send()

        @pl.when(jnp.logical_not(own_right))
        def _():
            pass_right(part, 0).wait_send()

    @pl.when(own_right)
    def _():
        remote(k_send, r_recv, s_r, r_r, mate).wait_send()


def store(pair_in, atoms_in, pair_to, atoms_to, done):
    first = pltpu.make_async_copy(pair_in, pair_to, done.at[0])
    second = pltpu.make_async_copy(atoms_in, atoms_to, done.at[1])
    first.start()
    second.start()
    first.wait()
    second.wait()


def per_device(
    pair, atoms, atom_token, tri_proj, tri_out, w_qkv, w_attn_out, w_token, w_row, w_col
):
    vmem = pl.BlockSpec(memory_space=pltpu.VMEM)
    sem = pltpu.SemaphoreType.DMA
    arguments = (
        pair, atoms, atom_token.reshape(1, 128), tri_proj, tri_out, w_qkv, w_attn_out, w_token,
        w_row, w_col,
    )
    results = pl.pallas_call(
        kernel,
        out_shape=(pltpu.VMEM(pair.shape, BF16), pltpu.VMEM(atoms.shape, BF16)),
        in_specs=[pl.BlockSpec(memory_space=pltpu.HBM)] * 10,
        out_specs=(vmem, vmem),
        scratch_shapes=[
            pltpu.VMEM(pair.shape, BF16),
            pltpu.VMEM(atoms.shape, BF16),
            pltpu.VMEM((1, 128), jnp.int32),
            pltpu.VMEM(tri_proj.shape, BF16),
            pltpu.VMEM(tri_out.shape, BF16),
            pltpu.VMEM(w_qkv.shape, BF16),
            pltpu.VMEM(w_attn_out.shape, BF16),
            pltpu.VMEM(w_token.shape, BF16),
            pltpu.VMEM(w_row.shape, BF16),
            pltpu.VMEM(w_col.shape, BF16),
            pltpu.VMEM((512, C), F32),
            pltpu.VMEM((32, 16, C), BF16),
            pltpu.VMEM((32, 16, C), BF16),
            pltpu.VMEM((2, 4, 64, C), BF16),
            pltpu.VMEM((4, 64, C), BF16),
            pltpu.VMEM((4, 4, 64, C), BF16),
            pltpu.VMEM((32, 8, C), BF16),
            pltpu.VMEM((32, 8, C), BF16),
            pltpu.VMEM((256, C), F32),
            pltpu.VMEM((256, C), F32),
            pltpu.VMEM((48, C), BF16),
            pltpu.VMEM((48, C), BF16),
            pltpu.VMEM((1, 128), jnp.int32),
            pltpu.VMEM((1, 128), jnp.int32),
            pltpu.VMEM((2, 2, 16, 8, C), BF16),
            pltpu.VMEM((64, 8, C), BF16),
            pltpu.VMEM((8, C), BF16),
            pltpu.VMEM((16, 8, C), BF16),
            pltpu.VMEM((8, C), BF16),
            sem((4,)), sem((4,)),
            sem, sem,
            sem((16,)), sem((16,)),
            sem, sem,
            sem, sem,
            sem, sem,
            sem, sem,
            sem, sem,
            sem((10,)),
            pltpu.SemaphoreType.REGULAR,
        ],
        compiler_params=pltpu.CompilerParams(
            collective_id=0, has_side_effects=True, vmem_limit_bytes=32 << 20
        ),
    )(*(pltpu.with_memory_space_constraint(value, pltpu.HBM) for value in arguments))
    hbm = pl.BlockSpec(memory_space=pltpu.HBM)
    return pl.pallas_call(
        store,
        out_shape=(
            jax.ShapeDtypeStruct(pair.shape, BF16),
            jax.ShapeDtypeStruct(atoms.shape, BF16),
        ),
        in_specs=[vmem, vmem],
        out_specs=(hbm, hbm),
        scratch_shapes=[sem((2,))],
    )(*(pltpu.with_memory_space_constraint(value, pltpu.VMEM) for value in results))


def solution(mesh):
    return jax.shard_map(
        per_device,
        mesh=mesh,
        in_specs=(
            P("row", "col", None),
            P("row", None),
            P("row"),
            P(),
            P(),
            P(),
            P(),
            P(),
            P(),
            P(),
        ),
        out_specs=(P("row", "col", None), P("row", None)),
        check_vma=False,
    )
```
